32 devices in a mesh: groups: 1, expert: 32 (over z, y, x, core).
Axes of the slice: x: 2, y: 2, z: 4, core: 2. Of those that a mesh axis runs over, the one named last changes fastest.
Arguments:
- hidden: bfloat16 [512, 7168], P(('groups', 'expert')), may hold values from -6 to 6
- expert_ids: int32 [512, 2], P(('groups', 'expert')), may hold values from 0 to 3, all different within a row; in each aligned block of 8 rows (0 to 7, 8 to 15, ...) at most 8 rows name the same one
- route_weights: float32 [512, 2], P(('groups', 'expert')), may hold values from 0.1 to 1
- gate_weight: bfloat16 [32, 7168, 256], P('expert'), may hold values from -0.0625 to 0.0625
- up_weight: bfloat16 [32, 7168, 256], P('expert'), may hold values from -0.0625 to 0.0625
- down_weight: bfloat16 [32, 256, 7168], P('expert'), may hold values from -0.125 to 0.125
- queries: bfloat16 [512, 128, 576], P(('groups', 'expert')), may hold values from -100 to 100
- latent_cache: bfloat16 [512, 512, 576], P(('groups', 'expert')), may hold values from -16 to 16
- lengths: int32 [512], P(('groups', 'expert')), may hold values from 64 to 512, as said below
Outputs:
- routed: bfloat16 [512, 7168], P(('groups', 'expert'))
- attended: bfloat16 [512, 128, 512], P(('groups', 'expert'))
The draws below stay inside these ranges and needn't reach their ends.
Inputs may be any that keep to these rules, and one draw needn't show every extreme that they name: `expert_ids`: each row names 2 different experts. `lengths`: the first request holds 512 positions.
All inputs are finite; a program needn't handle non-finite values.
Results may differ from the reference program's by a relative error of at most 0.008.
Values may be sent and summed in bfloat16 or wider, within the bound.
No kernel may reach another device: no remote copies, remote signals or barrier semaphores. Data moves between devices by JAX's collectives and lax.ppermute only.
A program may use at most 128 MiB of HBM per device.

```python
import math
import jax
import jax.numpy as jnp
import numpy as np
from jax import lax

D = 7168
FF = 2048
HEADS = 128
LAT = 512
ROPE = 64
H_DEV = 256
TOPK = 2
MB = 2
REQ_DEV = 16
CTX = 512
SLICES = 8
EXPERTS = 4
PIECES = 32
REQS = 512


def draw_queries(key, part):
    key = jax.random.fold_in(key, 1)
    shape = (REQS, HEADS, LAT + ROPE)
    return jnp.clip(jax.random.normal(key, shape, jnp.float32), -5.0, 5.0).astype(jnp.bfloat16)


def draw_latent_cache(key, part):
    key = jax.random.fold_in(key, 2)
    shape = (REQS, CTX, LAT + ROPE)
    return jnp.clip(jax.random.normal(key, shape, jnp.float32), -5.0, 5.0).astype(jnp.bfloat16)


def draw_lengths(key, part):
    key = jax.random.fold_in(key, 5)
    raw_lengths = jax.random.randint(key, (REQS,), CTX // 8, CTX + 1, dtype=jnp.int32)
    return jnp.where(jnp.arange(REQS) == 0, CTX, raw_lengths).astype(jnp.int32)


def shard_levels(stream_key, dims, pieces, least, largest):
    gain, own = 1.0, jax.random.fold_in(stream_key, 6)
    for axis_at, parts in pieces:
        steps = jnp.exp(jax.random.uniform(jax.random.fold_in(own, axis_at), (parts,), jnp.float32, least / len(pieces), largest / len(pieces)))
        gain = gain * jnp.repeat(steps, dims[axis_at] // parts).reshape([-1 if axis == axis_at else 1 for axis in range(len(dims))])
    return gain


def routed_block(rng, own, number, rows, count, top, bound, lean):
    order = jax.random.permutation(rng, count)
    heavy_load, usual = portions_of(count, rows * top, bound, lean, True), portions_of(count, rows * top, bound, lean, False)
    places = jnp.arange(count)

    def named(tallies, rotation):
        used = int((tallies > 0).sum())
        fixed = max(1, used // 4)
        passed = fixed + (places - fixed + rotation * (used - fixed)) % max(1, count - fixed)
        return jnp.zeros((count,), jnp.int32).at[order[jnp.where(places < fixed, places, passed)]].set(jnp.asarray(tallies, jnp.int32))

    tallies = jnp.where(number % 4 == 0, named(heavy_load, number // 4), named(usual, number - number // 4 - 1))
    mixed = jax.random.permutation(jax.random.fold_in(own, 3), count)
    source_of, sink = mixed[0:count // 2 * 2:2], mixed[1:count // 2 * 2:2]
    margin = jnp.minimum(tallies[source_of] - 1, bound - tallies[sink]) // 2
    margin = jnp.where((source_of == order[0]) | (sink == order[0]) | (tallies[sink] == 0), 0, jnp.maximum(margin, 0))
    passed = jax.random.randint(jax.random.fold_in(own, 4), (count // 2,), 0, 1 << 20) % (margin + 1)
    tallies = tallies.at[source_of].add(-passed).at[sink].add(passed)
    labels = jnp.searchsorted(jnp.cumsum(tallies), jnp.arange(rows * top), side="right").astype(jnp.int32)
    listing = labels.reshape(top, rows).T
    listing = listing[jax.random.permutation(jax.random.fold_in(own, 1), rows)]
    rotation = jax.random.randint(jax.random.fold_in(own, 2), (rows, 1), 0, top)
    return jnp.take_along_axis(listing, (jnp.arange(top)[None, :] + rotation) % top, axis=1)


def portions_of(amount, total, reach, slope, full):
    loads = [(1 << 20) // math.isqrt(grade ** slope) + 1 for grade in range(1, amount + 1)]
    largest = reach if full else min(reach, max(-(-total // amount), total * loads[0] // sum(loads)))
    least = 1 if total - largest >= amount - 1 else 0
    holding, surplus = [largest] + [least] * (amount - 1), total - largest - least * (amount - 1)
    while surplus > 0:
        candidates = [i for i in range(1, amount) if holding[i] < largest] or [i for i in range(1, amount) if holding[i] < reach]
        whole, remaining = sum([loads[i] for i in candidates]), surplus
        for i in candidates:
            addition = min(reach - holding[i], max(1, remaining * loads[i] // whole), surplus)
            holding[i] = holding[i] + addition
            surplus = surplus - addition
    return np.array(holding)


def scatter_about(key, dims, spread, limit, split=(), held_as=jnp.bfloat16):
    result = spread * jax.random.normal(key, dims, jnp.float32)
    if split:
        result = result * shard_levels(key, dims, split, -0.22, 0.18)
    return jnp.clip(result, -limit, limit).astype(held_as)


def setup_inputs(seed: int = 0, part: int = 0) -> dict:
    arg_keys = jax.random.split(jax.random.key(seed), 10)
    part_splits = jax.random.split(jax.random.fold_in(arg_keys[9], part), 10)
    hidden = scatter_about(part_splits[0], (REQS, D), 1.0, 6.0, ((0, 32),))
    expert_ids_keys = jax.random.split(jax.random.fold_in(part_splits[1], 1), REQS // (REQ_DEV // MB))
    expert_ids_turns = jax.random.permutation(jax.random.fold_in(part_splits[1], 3), REQS // (REQ_DEV // MB))
    expert_ids = jax.vmap(lambda own, number: routed_block(jax.random.fold_in(part_splits[1], 2), own, number, REQ_DEV // MB, EXPERTS, TOPK, REQ_DEV // MB, 2))(expert_ids_keys, expert_ids_turns).reshape((REQS, TOPK))
    route_weights = jnp.clip(0.1 + 0.9 * jax.random.uniform(part_splits[2], (REQS, TOPK), jnp.float32) ** shard_levels(part_splits[2], (REQS, TOPK), ((0, 32),), -0.2, 0.2), 0.1, 1.0)
    gate_weight = scatter_about(arg_keys[3], (PIECES, D, H_DEV), D ** -0.5, 0.0625, ((0, 32),))
    up_weight = scatter_about(arg_keys[4], (PIECES, D, H_DEV), D ** -0.5, 0.0625, ((0, 32),))
    down_weight = scatter_about(arg_keys[5], (PIECES, H_DEV, D), FF ** -0.5, 0.125, ((0, 32),))
    queries = draw_queries(jax.random.fold_in(jax.random.fold_in(arg_keys[9], part), 71), part)
    latent_cache = draw_latent_cache(jax.random.fold_in(jax.random.fold_in(arg_keys[9], part), 71), part)
    lengths = draw_lengths(jax.random.fold_in(jax.random.fold_in(arg_keys[9], part), 71), part)
    return dict(hidden=hidden, expert_ids=expert_ids, route_weights=route_weights, gate_weight=gate_weight, up_weight=up_weight, down_weight=down_weight, queries=queries, latent_cache=latent_cache, lengths=lengths)


score_scale = 0.07216878364870322


def expert_outputs(hidden, gate_weight, up_weight, down_weight):
    gate_full = gate_weight.reshape(EXPERTS, SLICES, D, H_DEV).transpose(0, 2, 1, 3).reshape(EXPERTS, D, FF)
    up_full = up_weight.reshape(EXPERTS, SLICES, D, H_DEV).transpose(0, 2, 1, 3).reshape(EXPERTS, D, FF)
    down_full = down_weight.reshape(EXPERTS, FF, D)

    def one_expert(matrices):
        gate_value = jnp.dot(hidden, matrices[0], preferred_element_type=jnp.float32)
        up_value = jnp.dot(hidden, matrices[1], preferred_element_type=jnp.float32)
        inner_value = (jax.nn.silu(gate_value) * up_value).astype(jnp.bfloat16)
        return jnp.dot(inner_value, matrices[2], preferred_element_type=jnp.float32)

    return lax.map(one_expert, (gate_full, up_full, down_full))


def reference(hidden, expert_ids, route_weights, gate_weight, up_weight, down_weight, queries, latent_cache, lengths):
    outputs = expert_outputs(hidden, gate_weight, up_weight, down_weight)
    choose = (expert_ids[:, :, None] == jnp.arange(EXPERTS, dtype=jnp.int32)[None, None, :]).astype(jnp.float32)
    mixing = jnp.sum(route_weights[:, :, None] * choose, axis=1)
    routed = jnp.einsum('re,erd->rd', mixing, outputs, precision=lax.Precision.HIGHEST).astype(jnp.bfloat16)
    query_full = queries.astype(jnp.float32)
    cache_full = latent_cache.astype(jnp.float32)
    scores = jnp.einsum('rhc,rpc->rhp', query_full, cache_full, precision=lax.Precision.HIGHEST) * score_scale
    positions = jnp.arange(CTX, dtype=jnp.int32)
    in_range = positions[None, None, :] < lengths[:, None, None]
    masked = jnp.where(in_range, scores, -jnp.inf)
    row_peak = jnp.max(masked, axis=-1, keepdims=True)
    raised = jnp.exp(masked - row_peak)
    weights = (raised / jnp.sum(raised, axis=-1, keepdims=True)).astype(jnp.bfloat16)
    attended = jnp.einsum('rhp,rpc->rhc', weights.astype(jnp.float32), cache_full[:, :, :LAT], precision=lax.Precision.HIGHEST).astype(jnp.bfloat16)
    return (routed, attended)
```

```python
import functools

import jax
import jax.numpy as jnp
from jax import lax
from jax.experimental import pallas as pl
from jax.experimental.pallas import tpu as pltpu
from jax.sharding import PartitionSpec as P

LAT = 512
SLICES = 8
AXIS = "expert"

score_scale = 0.07216878364870322


def attend_kernel(lengths_ref, queries_ref, cache_ref, out_ref):
    request = pl.program_id(0)
    length = lengths_ref[request]
    cache = cache_ref[0]
    scores = (
        lax.dot_general(
            queries_ref[0], cache, (((1,), (1,)), ((), ())), preferred_element_type=jnp.float32
        )
        * score_scale
    )
    positions = lax.broadcasted_iota(jnp.int32, scores.shape, 1)
    masked = jnp.where(positions < length, scores, -jnp.inf)
    row_peak = jnp.max(masked, axis=-1, keepdims=True)
    raised = jnp.exp(masked - row_peak)
    weights = (raised / jnp.sum(raised, axis=-1, keepdims=True)).astype(jnp.bfloat16)
    out_ref[0] = jnp.dot(
        weights, cache[:, :LAT], preferred_element_type=jnp.float32
    ).astype(jnp.bfloat16)


def attend(queries, latent_cache, lengths):
    requests, heads, width = queries.shape
    context = latent_cache.shape[1]
    return pl.pallas_call(
        attend_kernel,
        grid_spec=pltpu.PrefetchScalarGridSpec(
            num_scalar_prefetch=1,
            grid=(requests,),
            in_specs=[
                pl.BlockSpec((1, heads, width), lambda i, _: (i, 0, 0)),
                pl.BlockSpec((1, context, width), lambda i, _: (i, 0, 0)),
            ],
            out_specs=pl.BlockSpec((1, heads, LAT), lambda i, _: (i, 0, 0)),
        ),
        out_shape=jax.ShapeDtypeStruct((requests, heads, LAT), jnp.bfloat16),
        compiler_params=pltpu.CompilerParams(vmem_limit_bytes=24 * 1024 * 1024),
        cost_estimate=pl.CostEstimate(
            flops=2 * requests * heads * context * (width + LAT),
            bytes_accessed=2 * requests * (context * width + heads * (width + LAT)),
            transcendentals=requests * heads * context,
        ),
        name="latent_attention",
    )(lengths, queries, latent_cache)


def on_device(
    hidden,
    expert_ids,
    route_weights,
    gate_weight,
    up_weight,
    down_weight,
    queries,
    latent_cache,
    lengths,
):
    devices = lax.axis_size(AXIS)
    planes = devices // SLICES
    me = lax.axis_index(AXIS)
    core, plane, place = me % 2, me // SLICES, (me // 2) % 4
    rows, width = hidden.shape
    half, quarter = width // 2, width // 4
    first_core = core == 0

    def swap(value, bit):
        return lax.ppermute(value, AXIS, [(i, i ^ bit) for i in range(devices)])

    def shift(value, by):
        return lax.ppermute(
            value, AXIS, [(i, (i + SLICES * by) % devices) for i in range(devices)]
        )

    in_core = functools.partial(swap, bit=1)
    in_x = functools.partial(swap, bit=2)
    in_y = functools.partial(swap, bit=4)

    low, high = hidden[:, :half], hidden[:, half:]
    kept = jnp.where(first_core, low, high)
    got = in_core(jnp.where(first_core, high, low))
    block = jnp.where(
        first_core, jnp.concatenate([kept, got], 0), jnp.concatenate([got, kept], 0)
    )
    slots = [block] + [None] * (planes - 1)
    order = [k for k in (1, planes - 1) if k > 0] + list(range(2, planes - 1))
    for k in dict.fromkeys(order):
        slots[k] = shift(block, k)
    order = list(dict.fromkeys([0] + order))
    groups = [order[: planes // 2], order[planes // 2 :]]

    gate_part, up_part, down_part = gate_weight[0], up_weight[0], down_weight[0]
    other = (1 - core) * half
    gate_own = lax.dynamic_slice_in_dim(gate_part, core * half, half, 0)
    up_own = lax.dynamic_slice_in_dim(up_part, core * half, half, 0)
    entry_other = in_core(
        jnp.concatenate(
            [
                lax.dynamic_slice_in_dim(gate_part, other, half, 0),
                lax.dynamic_slice_in_dim(up_part, other, half, 0),
            ],
            1,
        )
    )
    entry_own = jnp.concatenate([gate_own, up_own], 1)
    down_own = jnp.where(first_core, down_part[:, :half], down_part[:, half:])
    down_other = in_core(jnp.where(first_core, down_part[:, half:], down_part[:, :half]))
    down_both = jnp.concatenate([down_own, down_other], 0)
    hidden_units = gate_part.shape[1]

    choose = (
        expert_ids[:, :, None] == jnp.arange(planes, dtype=jnp.int32)[None, None, :]
    ).astype(jnp.float32)
    mixing = jnp.sum(route_weights[:, :, None] * choose, axis=1)
    mixing_all = lax.all_gather(mixing, AXIS, axis=0, tiled=True)
    mine = jnp.sum(
        jnp.where(jnp.arange(planes)[None, :] == plane, mixing_all, 0.0), axis=1
    ).reshape(planes, 4, 2 * rows)

    def arrival_mixing(group):
        source_plane = (plane - jnp.array(group) + planes) % planes
        source_place = jnp.arange(4) ^ place
        pick_plane = source_plane[:, None] == jnp.arange(planes)[None, :]
        pick_place = source_place[:, None] == jnp.arange(4)[None, :]
        pick = pick_place[:, None, None, :] & pick_plane[None, :, :, None]
        chosen = jnp.where(pick[..., None], mine[None, None], 0.0)
        return jnp.sum(chosen, axis=(2, 3)).reshape(-1, 1)

    attended = attend(queries, latent_cache, lengths)

    def gather_plane(group):
        part_a = jnp.stack([slots[k][:, :quarter] for k in group])
        part_b = jnp.stack([slots[k][:, quarter:] for k in group])
        pair_a = jnp.stack([part_a, in_x(part_a)])
        pair_b = jnp.stack([part_b, in_y(part_b)])
        four_a = jnp.stack([pair_a, in_y(pair_a)])
        four_b = jnp.stack([pair_b, in_x(pair_b)], 1)
        return jnp.concatenate([four_a, four_b], -1).reshape(-1, half)

    def inner_of(arrived):
        pre_other = jnp.dot(arrived, entry_other, preferred_element_type=jnp.float32)
        pre_own = jnp.dot(arrived, entry_own, preferred_element_type=jnp.float32)
        pre = pre_own + in_core(pre_other)
        gate_value, up_value = pre[:, :hidden_units], pre[:, hidden_units:]
        inner = (jax.nn.silu(gate_value) * up_value).astype(jnp.bfloat16)
        return jnp.concatenate([inner, in_core(inner)], 1)

    def narrow(value):
        return value.astype(jnp.bfloat16)

    def widen(value):
        return value.astype(jnp.float32)

    def sum_plane(partial, group):
        partial = partial.reshape(2, 2, len(group), 2 * rows, half)
        part_a, part_b = partial[..., :quarter], partial[..., quarter:]
        pair_a = part_a[0] + widen(in_y(narrow(part_a[1])))
        pair_b = part_b[:, 0] + widen(in_x(narrow(part_b[:, 1])))
        one_a = pair_a[0] + widen(in_x(narrow(pair_a[1])))
        one_b = pair_b[0] + widen(in_y(narrow(pair_b[1])))
        return jnp.concatenate([one_a, one_b], -1)

    arrived = [gather_plane(group) for group in groups]
    inner = [inner_of(value) for value in arrived]
    total = None
    for group, value in reversed(list(zip(groups, inner))):
        partial = jnp.dot(value, down_both, preferred_element_type=jnp.float32)
        sums = sum_plane(partial * arrival_mixing(group), group)
        for at, k in enumerate(group):
            term = sums[at] if k == 0 else widen(shift(narrow(sums[at]), -k))
            total = term if total is None else total + term

    result = narrow(total)
    top, bottom = result[:rows], result[rows:]
    kept = jnp.where(first_core, top, bottom)
    got = in_core(jnp.where(first_core, bottom, top))
    routed = jnp.where(
        first_core, jnp.concatenate([kept, got], 1), jnp.concatenate([got, kept], 1)
    )
    return routed, attended


def solution(mesh):
    in_specs = (
        P(("groups", "expert"), None),
        P(("groups", "expert"), None),
        P(("groups", "expert"), None),
        P("expert", None, None),
        P("expert", None, None),
        P("expert", None, None),
        P(("groups", "expert"), None, None),
        P(("groups", "expert"), None, None),
        P(("groups", "expert")),
    )
    out_specs = (P(("groups", "expert"), None), P(("groups", "expert"), None, None))
    return jax.shard_map(
        on_device, mesh=mesh, in_specs=in_specs, out_specs=out_specs, check_vma=False
    )
```

```python
import functools
import math

import jax
import jax.numpy as jnp
from jax import lax
from jax.experimental import pallas as pl
from jax.experimental.pallas import tpu as pltpu
from jax.sharding import PartitionSpec as P

LAT = 512
SLICES = 8
AXIS = "expert"
ATTEND_CALLS = 4
ATTEND_TOGETHER = 4

score_scale = 0.07216878364870322

SMALL = pl.CostEstimate(flops=1, bytes_accessed=1, transcendentals=0)


def attend_kernel(lengths_ref, queries_ref, cache_ref, *refs, first):
    out_ref = refs[-1]
    each = out_ref.shape[0]
    masked = []
    for at in range(each):
        length = lengths_ref[first + pl.program_id(0) * each + at]
        scores = lax.dot_general(
            queries_ref[at],
            cache_ref[at],
            (((0,), (0,)), ((), ())),
            preferred_element_type=jnp.float32,
        )
        positions = lax.broadcasted_iota(jnp.int32, scores.shape, 1)
        masked.append(jnp.where(positions < length, scores * score_scale, -jnp.inf))
    weights = []
    for scores in masked:
        raised = jnp.exp(scores - jnp.max(scores, axis=-1, keepdims=True))
        weights.append((raised / jnp.sum(raised, axis=-1, keepdims=True)).astype(jnp.bfloat16))
    for at in range(each):
        out_ref[at] = lax.dot_general(
            weights[at],
            cache_ref[at, :LAT],
            (((1,), (1,)), ((), ())),
            preferred_element_type=jnp.float32,
        ).astype(jnp.bfloat16)


def attend(queries, latent_cache, lengths, first, count, held):
    requests, width, heads = queries.shape
    context = latent_cache.shape[2]
    aliases = {} if held is None else {3: 0}
    operands = (lengths, queries, latent_cache) + (() if held is None else (held,))
    each = math.gcd(count, ATTEND_TOGETHER)
    block = first // each
    return pl.pallas_call(
        functools.partial(attend_kernel, first=first),
        grid_spec=pltpu.PrefetchScalarGridSpec(
            num_scalar_prefetch=1,
            grid=(count // each,),
            in_specs=[
                pl.BlockSpec((each, width, heads), lambda i, _: (block + i, 0, 0)),
                pl.BlockSpec((each, width, context), lambda i, _: (block + i, 0, 0)),
            ]
            + ([] if held is None else [pl.BlockSpec(memory_space=pl.ANY)]),
            out_specs=pl.BlockSpec((each, heads, LAT), lambda i, _: (block + i, 0, 0)),
        ),
        out_shape=jax.ShapeDtypeStruct((requests, heads, LAT), jnp.bfloat16),
        input_output_aliases=aliases,
        compiler_params=pltpu.CompilerParams(vmem_limit_bytes=20 * 1024 * 1024),
        cost_estimate=SMALL,
        name="latent_attention",
    )(*operands)


def tile_of(half):
    return half // next(n for n in (7, 4, 2, 1) if half % (n * 128) == 0)


def entry_half_kernel(_, gate_ref, up_ref, out_ref):
    out_ref[0] = gate_ref[...]
    out_ref[1] = up_ref[...]


def entry_half(core, gate, up):
    width, units = gate.shape
    tile = tile_of(width // 2)
    steps = width // 2 // tile
    spec = pl.BlockSpec((tile, units), lambda i, core: ((1 - core[0]) * steps + i, 0))
    return pl.pallas_call(
        entry_half_kernel,
        grid_spec=pltpu.PrefetchScalarGridSpec(
            num_scalar_prefetch=1,
            grid=(steps,),
            in_specs=[spec, spec],
            out_specs=pl.BlockSpec((2, tile, units), lambda i, core: (0, i, 0)),
        ),
        out_shape=jax.ShapeDtypeStruct((2, width // 2, units), gate.dtype),
        compiler_params=pltpu.CompilerParams(vmem_limit_bytes=48 * 1024 * 1024),
        cost_estimate=SMALL,
        name="entry_half",
    )(core.reshape(1), gate, up)


def exit_half_kernel(_, given_ref, kept_ref, given_out_ref, kept_out_ref):
    given_out_ref[...] = given_ref[...]
    kept_out_ref[...] = kept_ref[...]


def exit_half(core, down):
    units, width = down.shape
    tile = tile_of(width // 2)
    steps = width // 2 // tile
    shape = jax.ShapeDtypeStruct((units, width // 2), down.dtype)
    return pl.pallas_call(
        exit_half_kernel,
        grid_spec=pltpu.PrefetchScalarGridSpec(
            num_scalar_prefetch=1,
            grid=(steps,),
            in_specs=[
                pl.BlockSpec((units, tile), lambda i, core: (0, (1 - core[0]) * steps + i)),
                pl.BlockSpec((units, tile), lambda i, core: (0, core[0] * steps + i)),
            ],
            out_specs=[pl.BlockSpec((units, tile), lambda i, core: (0, i))] * 2,
        ),
        out_shape=[shape, shape],
        compiler_params=pltpu.CompilerParams(vmem_limit_bytes=16 * 1024 * 1024),
        cost_estimate=SMALL,
        name="exit_half",
    )(core.reshape(1), down, down)


def entry_kernel(_, rows_ref, gate_ref, up_ref, out_ref):
    @pl.when(pl.program_id(0) == 0)
    def _():
        out_ref[...] = jnp.zeros_like(out_ref)

    rows = rows_ref[...]
    out_ref[0] += jnp.dot(rows, gate_ref[...], preferred_element_type=jnp.float32)
    out_ref[1] += jnp.dot(rows, up_ref[...], preferred_element_type=jnp.float32)


def entry(rows, core, gate, up):
    count, half = rows.shape
    units = gate.shape[-1]
    steps = next(n for n in (7, 4, 2, 1) if half % (n * 128) == 0)
    tile = half // steps
    if gate.ndim == 3:
        specs = [
            pl.BlockSpec((None, tile, units), lambda i, core: (0, i, 0)),
            pl.BlockSpec((None, tile, units), lambda i, core: (1, i, 0)),
        ]
    else:
        specs = [pl.BlockSpec((tile, units), lambda i, core: (core[0] * steps + i, 0))] * 2
    return pl.pallas_call(
        entry_kernel,
        grid_spec=pltpu.PrefetchScalarGridSpec(
            num_scalar_prefetch=1,
            grid=(steps,),
            in_specs=[pl.BlockSpec((count, tile), lambda i, core: (0, i))] + specs,
            out_specs=pl.BlockSpec((2, count, units), lambda i, core: (0, 0, 0)),
        ),
        out_shape=jax.ShapeDtypeStruct((2, count, units), jnp.float32),
        compiler_params=pltpu.CompilerParams(vmem_limit_bytes=16 * 1024 * 1024),
        cost_estimate=SMALL,
        name="entry_products",
    )(core.reshape(1), rows, gate, up)


def inner_kernel(own_ref, other_ref, out_ref):
    gate_value = own_ref[0] + other_ref[0]
    up_value = own_ref[1] + other_ref[1]
    silu = gate_value / (1.0 + jnp.exp(-gate_value))
    out_ref[...] = (silu * up_value).astype(out_ref.dtype)


def inner_units(own, other):
    return pl.pallas_call(
        inner_kernel,
        in_specs=[pl.BlockSpec(memory_space=pltpu.VMEM)] * 2,
        out_specs=pl.BlockSpec(memory_space=pltpu.VMEM),
        out_shape=jax.ShapeDtypeStruct(own.shape[1:], jnp.bfloat16),
        compiler_params=pltpu.CompilerParams(vmem_limit_bytes=12 * 1024 * 1024),
        cost_estimate=SMALL,
        name="inner_units",
    )(own, other)


def exit_kernel(own_ref, other_ref, down_own_ref, down_other_ref, *out_refs, rows):
    own, other = own_ref[...], other_ref[...]
    quarter = down_own_ref.shape[1] // 2
    tile = math.gcd(quarter, 256)
    for at in range(2 * quarter // tile):
        columns = slice(at * tile, (at + 1) * tile)
        part = jnp.dot(own, down_own_ref[:, columns], preferred_element_type=jnp.float32)
        part += jnp.dot(other, down_other_ref[:, columns], preferred_element_type=jnp.float32)
        second = at * tile >= quarter
        begin = at * tile - (quarter if second else 0)
        columns = slice(begin, begin + tile)
        row = 0
        for first in range(0, len(out_refs), 4):
            kept_a, kept_b, sent_a, sent_b = out_refs[first : first + 4]
            for slot in range(kept_a.shape[1]):
                for y in range(2):
                    for x in range(2):
                        value = part[row : row + rows]
                        row += rows
                        if second:
                            target = sent_b if x else kept_b
                            target[y, slot, :, columns] = value.astype(target.dtype)
                        else:
                            target = sent_a if y else kept_a
                            target[x, slot, :, columns] = value.astype(target.dtype)


def exit_sums(own, other, down_own, down_other, rows, sets):
    quarter = down_own.shape[1] // 2
    shapes = []
    for slots in sets:
        shape = (2, slots, rows, quarter)
        shapes += [jax.ShapeDtypeStruct(shape, jnp.float32)] * 2
        shapes += [jax.ShapeDtypeStruct(shape, jnp.bfloat16)] * 2
    outs = pl.pallas_call(
        functools.partial(exit_kernel, rows=rows),
        in_specs=[pl.BlockSpec(memory_space=pltpu.VMEM)] * 4,
        out_specs=[pl.BlockSpec(memory_space=pltpu.VMEM)] * len(shapes),
        out_shape=shapes,
        compiler_params=pltpu.CompilerParams(vmem_limit_bytes=16 * 1024 * 1024),
        cost_estimate=SMALL,
        name="exit_sums",
    )(own, other, down_own, down_other)
    return [
        (tuple(outs[at : at + 2]), tuple(outs[at + 2 : at + 4])) for at in range(0, len(outs), 4)
    ]


def after(value, *others):
    return lax.optimization_barrier((value,) + others)[0]


def on_device(
    hidden,
    expert_ids,
    route_weights,
    gate_weight,
    up_weight,
    down_weight,
    queries,
    latent_cache,
    lengths,
):
    devices = lax.axis_size(AXIS)
    planes = devices // SLICES
    me = lax.axis_index(AXIS)
    core, plane = me % 2, me // SLICES
    rows, width = hidden.shape
    half, quarter = width // 2, width // 4
    first_core = core == 0

    def swap(value, bit):
        return lax.ppermute(value, AXIS, [(i, i ^ bit) for i in range(devices)])

    def shift(value, by):
        return lax.ppermute(
            value, AXIS, [(i, (i + SLICES * by) % devices) for i in range(devices)]
        )

    in_core = functools.partial(swap, bit=1)
    in_x = functools.partial(swap, bit=2)
    in_y = functools.partial(swap, bit=4)

    low, high = hidden[:, :half], hidden[:, half:]
    kept = jnp.where(first_core, low, high)
    got = in_core(jnp.where(first_core, high, low))
    block = jnp.where(
        first_core, jnp.concatenate([kept, got], 0), jnp.concatenate([got, kept], 0)
    )
    choose = (
        expert_ids[:, :, None] == jnp.arange(planes, dtype=jnp.int32)[None, None, :]
    ).astype(jnp.float32)
    mixing = jnp.sum(route_weights[:, :, None] * choose, axis=1)
    mixing_other = in_core(mixing)
    mixing = jnp.where(
        first_core,
        jnp.concatenate([mixing, mixing_other], 0),
        jnp.concatenate([mixing_other, mixing], 0),
    )

    def mixing_of(expert):
        pick = jnp.arange(planes)[None, :] == expert
        return jnp.sum(jnp.where(pick, mixing, 0.0), axis=1, keepdims=True)

    queries_turned = jnp.swapaxes(queries, 1, 2)
    cache_turned = jnp.swapaxes(latent_cache, 1, 2)
    step = rows // ATTEND_CALLS

    def attend_more(number, held, *others):
        return attend(
            queries_turned, cache_turned, after(lengths, *others), number * step, step, held
        )

    def spread_first(slots):
        part_a = jnp.stack([slot[:, :quarter] for slot in slots])
        part_b = jnp.stack([slot[:, quarter:] for slot in slots])
        return (part_a, part_b), (in_x(part_a), in_y(part_b))

    def spread_second(held, got):
        pair_a = jnp.stack([held[0], got[0]])
        pair_b = jnp.stack([held[1], got[1]])
        return (pair_a, pair_b), (in_y(pair_a), in_x(pair_b))

    def spread_rows(held, got):
        four_a = jnp.stack([held[0], got[0]])
        four_b = jnp.stack([held[1], got[1]], 1)
        four = jnp.concatenate([four_a, four_b], -1)
        return jnp.moveaxis(four, 2, 0).reshape(-1, half)

    def narrow(value):
        return value.astype(jnp.bfloat16)

    def widen(value):
        return value.astype(jnp.float32)

    gate_part, up_part, down_part = gate_weight[0], up_weight[0], down_weight[0]

    def gather_second(kept, got):
        pair_a, pair_b = kept[0] + widen(got[0]), kept[1] + widen(got[1])
        return (pair_a[0], pair_b[0]), (narrow(pair_a[1]), narrow(pair_b[1]))

    def gather_rows(kept, got):
        return jnp.concatenate([kept[0] + widen(got[0]), kept[1] + widen(got[1])], -1)

    def returned(sums, slots):
        return [
            (k, sums[at] if k == 0 else shift(narrow(sums[at]), -k))
            for at, k in enumerate(slots)
        ]

    near, far = list(range(1, planes - 1)), [planes - 1]
    join = lax.optimization_barrier

    slot_near = [shift(block, k) for k in near]
    held, got = spread_first([block])
    core, _ = join((core, block))
    entry_give = entry_half(core, gate_part, up_part)
    held, got, entry_give = join((held, got, entry_give))

    entry_other = in_core(entry_give)
    own, own_got = spread_second(held, got)
    attended = attend_more(0, None, entry_give)
    own, own_got, slot_near, attended, block = join((own, own_got, slot_near, attended, block))

    slot_far = [shift(block, k) for k in far]
    held, got = spread_first(slot_near)
    attended = attend_more(1, attended, block)
    held, got, slot_far, attended = join((held, got, slot_far, attended))

    near_held, near_got = spread_second(held, got)
    held, got = spread_first(slot_far)
    attended = attend_more(2, attended, *slot_far)
    down_give, down_own = exit_half(after(core, *slot_far), down_part)
    near_held, near_got, held, got, attended, down_give, down_own = join(
        (near_held, near_got, held, got, attended, down_give, down_own)
    )
    down_other = in_core(down_give)

    far_held, far_got = spread_second(held, got)
    arrived = jnp.concatenate(
        [spread_rows(own, own_got), spread_rows(near_held, near_got)], 0
    )
    pre_other = in_core(entry(arrived, core, entry_other, entry_other))
    pre_own = entry(arrived, core, gate_part, up_part)
    far_held, far_got, pre_own = join((far_held, far_got, pre_own))

    inner = inner_units(pre_own, pre_other)
    inner_other = in_core(inner)
    (own_kept, own_sent), (near_kept, near_sent) = exit_sums(
        inner, inner_other, down_own, down_other, 2 * rows, [1, len(near)]
    )
    near_sent, far_held, far_got = join((near_sent, far_held, far_got))

    near_got = (in_y(near_sent[0]), in_x(near_sent[1]))
    arrived = spread_rows(far_held, far_got)
    pre_other = in_core(entry(arrived, core, entry_other, entry_other))
    pre_own = entry(arrived, core, gate_part, up_part)
    near_kept, near_got, pre_own, pre_other, attended = join(
        (near_kept, near_got, pre_own, pre_other, attended)
    )

    near_kept, near_sent = gather_second(near_kept, near_got)
    near_got = (in_x(near_sent[0]), in_y(near_sent[1]))
    inner = inner_units(pre_own, pre_other)
    inner_other = in_core(inner)
    [(far_kept, far_sent)] = exit_sums(
        inner, inner_other, down_own, down_other, 2 * rows, [len(far)]
    )
    rest_sent = tuple(jnp.concatenate(pair, 1) for pair in zip(far_sent, own_sent))
    rest_kept = tuple(jnp.concatenate(pair, 1) for pair in zip(far_kept, own_kept))
    near_kept, near_got, rest_kept, rest_sent = join((near_kept, near_got, rest_kept, rest_sent))

    terms = returned(gather_rows(near_kept, near_got), near)
    rest_got = (in_y(rest_sent[0]), in_x(rest_sent[1]))
    attended = attend_more(3, attended, *rest_sent)
    rest_kept, rest_got, attended = join((rest_kept, rest_got, attended))

    rest_kept, rest_sent = gather_second(rest_kept, rest_got)
    rest_got = (in_x(rest_sent[0]), in_y(rest_sent[1]))
    terms += returned(gather_rows(rest_kept, rest_got), far + [0])
    total = 0.0
    for k, term in terms:
        total = total + mixing_of((plane + k) % planes) * widen(term)

    result = narrow(total)
    top, bottom = result[:rows], result[rows:]
    kept = jnp.where(first_core, top, bottom)
    got = in_core(jnp.where(first_core, bottom, top))
    routed = jnp.where(
        first_core, jnp.concatenate([kept, got], 1), jnp.concatenate([got, kept], 1)
    )
    return routed, attended


def solution(mesh):
    in_specs = (
        P(("groups", "expert"), None),
        P(("groups", "expert"), None),
        P(("groups", "expert"), None),
        P("expert", None, None),
        P("expert", None, None),
        P("expert", None, None),
        P(("groups", "expert"), None, None),
        P(("groups", "expert"), None, None),
        P(("groups", "expert")),
    )
    out_specs = (P(("groups", "expert"), None), P(("groups", "expert"), None, None))
    return jax.shard_map(
        on_device, mesh=mesh, in_specs=in_specs, out_specs=out_specs, check_vma=False
    )
```

```python
import functools
import math

import jax
import jax.numpy as jnp
from jax import lax
from jax.experimental import pallas as pl
from jax.experimental.pallas import tpu as pltpu
from jax.sharding import PartitionSpec as P

LAT = 512
SLICES = 8
AXIS = "expert"
ATTEND_CALLS = 4
ATTEND_TOGETHER = 4

score_scale = 0.07216878364870322

SMALL = pl.CostEstimate(flops=1, bytes_accessed=1, transcendentals=0)


def attend_kernel(lengths_ref, queries_ref, cache_ref, *refs, first):
    out_ref = refs[-1]
    each = out_ref.shape[0]
    masked = []
    for at in range(each):
        length = lengths_ref[first + pl.program_id(0) * each + at]
        scores = lax.dot_general(
            queries_ref[at],
            cache_ref[at],
            (((0,), (0,)), ((), ())),
            preferred_element_type=jnp.float32,
        )
        positions = lax.broadcasted_iota(jnp.int32, scores.shape, 1)
        masked.append(jnp.where(positions < length, scores * score_scale, -jnp.inf))
    weights = []
    for scores in masked:
        raised = jnp.exp(scores - jnp.max(scores, axis=-1, keepdims=True))
        weights.append((raised / jnp.sum(raised, axis=-1, keepdims=True)).astype(jnp.bfloat16))
    for at in range(each):
        out_ref[at] = lax.dot_general(
            weights[at],
            cache_ref[at, :LAT],
            (((1,), (1,)), ((), ())),
            preferred_element_type=jnp.float32,
        ).astype(jnp.bfloat16)


def attend(queries, latent_cache, lengths, first, count, held):
    requests, width, heads = queries.shape
    context = latent_cache.shape[2]
    aliases = {} if held is None else {3: 0}
    operands = (lengths, queries, latent_cache) + (() if held is None else (held,))
    each = math.gcd(count, ATTEND_TOGETHER)
    block = first // each
    return pl.pallas_call(
        functools.partial(attend_kernel, first=first),
        grid_spec=pltpu.PrefetchScalarGridSpec(
            num_scalar_prefetch=1,
            grid=(count // each,),
            in_specs=[
                pl.BlockSpec((each, width, heads), lambda i, _: (block + i, 0, 0)),
                pl.BlockSpec((each, width, context), lambda i, _: (block + i, 0, 0)),
            ]
            + ([] if held is None else [pl.BlockSpec(memory_space=pl.ANY)]),
            out_specs=pl.BlockSpec((each, heads, LAT), lambda i, _: (block + i, 0, 0)),
        ),
        out_shape=jax.ShapeDtypeStruct((requests, heads, LAT), jnp.bfloat16),
        input_output_aliases=aliases,
        compiler_params=pltpu.CompilerParams(vmem_limit_bytes=20 * 1024 * 1024),
        cost_estimate=SMALL,
        name="latent_attention",
    )(*operands)


def tile_of(half):
    return half // next(n for n in (7, 4, 2, 1) if half % (n * 128) == 0)


def entry_half_kernel(_, gate_ref, up_ref, out_ref):
    out_ref[0] = gate_ref[...]
    out_ref[1] = up_ref[...]


def entry_half(core, gate, up):
    width, units = gate.shape
    steps = 2
    tile = width // 2 // steps
    spec = pl.BlockSpec((tile, units), lambda i, core: ((1 - core[0]) * steps + i, 0))
    return pl.pallas_call(
        entry_half_kernel,
        grid_spec=pltpu.PrefetchScalarGridSpec(
            num_scalar_prefetch=1,
            grid=(steps,),
            in_specs=[spec, spec],
            out_specs=pl.BlockSpec((2, tile, units), lambda i, core: (0, i, 0)),
        ),
        out_shape=jax.ShapeDtypeStruct((2, width // 2, units), gate.dtype),
        compiler_params=pltpu.CompilerParams(vmem_limit_bytes=16 * 1024 * 1024),
        cost_estimate=SMALL,
        name="entry_half",
    )(core.reshape(1), gate, up)


def hold_kernel(in_ref, out_ref):
    out_ref[0] = in_ref[0]


def hold(value):
    return pl.pallas_call(
        hold_kernel,
        in_specs=[pl.BlockSpec(memory_space=pltpu.SMEM)],
        out_specs=pl.BlockSpec(memory_space=pltpu.SMEM),
        out_shape=jax.ShapeDtypeStruct((1,), value.dtype),
        compiler_params=pltpu.CompilerParams(vmem_limit_bytes=1024 * 1024),
        cost_estimate=SMALL,
        name="hold",
    )(value.reshape(1))[0]


def exit_half_kernel(_, given_ref, kept_ref, given_out_ref, kept_out_ref):
    given_out_ref[...] = given_ref[...]
    kept_out_ref[...] = kept_ref[...]


def exit_half(core, down):
    units, width = down.shape
    tile = tile_of(width // 2)
    steps = width // 2 // tile
    shape = jax.ShapeDtypeStruct((units, width // 2), down.dtype)
    return pl.pallas_call(
        exit_half_kernel,
        grid_spec=pltpu.PrefetchScalarGridSpec(
            num_scalar_prefetch=1,
            grid=(steps,),
            in_specs=[
                pl.BlockSpec((units, tile), lambda i, core: (0, (1 - core[0]) * steps + i)),
                pl.BlockSpec((units, tile), lambda i, core: (0, core[0] * steps + i)),
            ],
            out_specs=[pl.BlockSpec((units, tile), lambda i, core: (0, i))] * 2,
        ),
        out_shape=[shape, shape],
        compiler_params=pltpu.CompilerParams(vmem_limit_bytes=16 * 1024 * 1024),
        cost_estimate=SMALL,
        name="exit_half",
    )(core.reshape(1), down, down)


def entry_kernel(core_ref, rows_ref, *refs):
    weight_refs, out_ref = refs[:-1], refs[-1]
    half = rows_ref.shape[1]
    rows = rows_ref[...]
    for which in range(2):
        if len(weight_refs) == 1:
            weight = weight_refs[0][which]
        else:
            begin = pl.multiple_of(core_ref[0] * half, half)
            weight = weight_refs[which][pl.ds(begin, half)]
        out_ref[which] = jnp.dot(rows, weight, preferred_element_type=jnp.float32)


def entry(rows, core, *weights):
    return pl.pallas_call(
        entry_kernel,
        in_specs=[pl.BlockSpec(memory_space=pltpu.SMEM)]
        + [pl.BlockSpec(memory_space=pltpu.VMEM)] * (1 + len(weights)),
        out_specs=pl.BlockSpec(memory_space=pltpu.VMEM),
        out_shape=jax.ShapeDtypeStruct((2, rows.shape[0], weights[0].shape[-1]), jnp.float32),
        compiler_params=pltpu.CompilerParams(vmem_limit_bytes=16 * 1024 * 1024),
        cost_estimate=SMALL,
        name="entry_products",
    )(core.reshape(1), rows, *weights)


def inner_kernel(own_ref, other_ref, out_ref):
    gate_value = own_ref[0] + other_ref[0]
    up_value = own_ref[1] + other_ref[1]
    silu = gate_value / (1.0 + jnp.exp(-gate_value))
    out_ref[...] = (silu * up_value).astype(out_ref.dtype)


def inner_units(own, other, vmem=12):
    return pl.pallas_call(
        inner_kernel,
        in_specs=[pl.BlockSpec(memory_space=pltpu.VMEM)] * 2,
        out_specs=pl.BlockSpec(memory_space=pltpu.VMEM),
        out_shape=jax.ShapeDtypeStruct(own.shape[1:], jnp.bfloat16),
        compiler_params=pltpu.CompilerParams(vmem_limit_bytes=vmem * 1024 * 1024),
        cost_estimate=SMALL,
        name="inner_units",
    )(own, other)


def exit_kernel(own_ref, other_ref, down_own_ref, down_other_ref, *out_refs, sets, rows, sent):
    quarter = down_own_ref.shape[1] // 2
    tile = math.gcd(quarter, 256)

    def picked(ref, second):
        strips = []
        for begin, slots in sets:
            for slot in range(slots):
                for other in range(2):
                    y, x = (other, sent) if second else (sent, other)
                    at = ((begin + slot) * 4 + y * 2 + x) * rows
                    strips.append(ref[at : at + rows])
        return jnp.concatenate(strips, 0)

    for second in range(2):
        own, other = picked(own_ref, second), picked(other_ref, second)
        for at in range(quarter // tile):
            source = slice(second * quarter + at * tile, second * quarter + (at + 1) * tile)
            columns = slice(at * tile, (at + 1) * tile)
            part = jnp.dot(own, down_own_ref[:, source], preferred_element_type=jnp.float32)
            part += jnp.dot(other, down_other_ref[:, source], preferred_element_type=jnp.float32)
            row = 0
            for number, (_, slots) in enumerate(sets):
                target = out_refs[2 * number + second]
                for slot in range(slots):
                    for which in range(2):
                        value = part[row : row + rows]
                        target[which, slot, :, columns] = value.astype(target.dtype)
                        row += rows


def exit_sums(inner, down, rows, sets, sent):
    quarter = down[0].shape[1] // 2
    dtype = jnp.bfloat16 if sent else jnp.float32
    shapes = []
    for _, slots in sets:
        shapes += [jax.ShapeDtypeStruct((2, slots, rows, quarter), dtype)] * 2
    outs = pl.pallas_call(
        functools.partial(exit_kernel, sets=sets, rows=rows, sent=int(sent)),
        in_specs=[pl.BlockSpec(memory_space=pltpu.VMEM)] * 4,
        out_specs=[pl.BlockSpec(memory_space=pltpu.VMEM)] * len(shapes),
        out_shape=shapes,
        compiler_params=pltpu.CompilerParams(vmem_limit_bytes=16 * 1024 * 1024),
        cost_estimate=SMALL,
        name="exit_sums",
    )(*inner, *down)
    return [tuple(outs[at : at + 2]) for at in range(0, len(outs), 2)]


def after(value, *others):
    return lax.optimization_barrier((value,) + others)[0]


def on_device(
    hidden,
    expert_ids,
    route_weights,
    gate_weight,
    up_weight,
    down_weight,
    queries,
    latent_cache,
    lengths,
):
    devices = lax.axis_size(AXIS)
    planes = devices // SLICES
    me = lax.axis_index(AXIS)
    core, plane = me % 2, me // SLICES
    rows, width = hidden.shape
    half, quarter = width // 2, width // 4
    first_core = core == 0

    def swap(value, bit):
        return lax.ppermute(value, AXIS, [(i, i ^ bit) for i in range(devices)])

    def shift(value, by):
        return lax.ppermute(
            value, AXIS, [(i, (i + SLICES * by) % devices) for i in range(devices)]
        )

    in_core = functools.partial(swap, bit=1)
    in_x = functools.partial(swap, bit=2)
    in_y = functools.partial(swap, bit=4)

    low, high = hidden[:, :half], hidden[:, half:]
    kept = jnp.where(first_core, low, high)
    got = in_core(jnp.where(first_core, high, low))
    block = jnp.where(
        first_core, jnp.concatenate([kept, got], 0), jnp.concatenate([got, kept], 0)
    )
    choose = (
        expert_ids[:, :, None] == jnp.arange(planes, dtype=jnp.int32)[None, None, :]
    ).astype(jnp.float32)
    mixing = jnp.sum(route_weights[:, :, None] * choose, axis=1)
    mixing_other = in_core(mixing)
    mixing = jnp.where(
        first_core,
        jnp.concatenate([mixing, mixing_other], 0),
        jnp.concatenate([mixing_other, mixing], 0),
    )

    def mixing_of(expert):
        pick = jnp.arange(planes)[None, :] == expert
        return jnp.sum(jnp.where(pick, mixing, 0.0), axis=1, keepdims=True)

    queries_turned = jnp.swapaxes(queries, 1, 2)
    cache_turned = jnp.swapaxes(latent_cache, 1, 2)
    step = rows // ATTEND_CALLS

    def attend_more(number, held, *others):
        return attend(
            queries_turned, cache_turned, after(lengths, *others), number * step, step, held
        )

    def spread_first(slots):
        part_a = jnp.stack([slot[:, :quarter] for slot in slots])
        part_b = jnp.stack([slot[:, quarter:] for slot in slots])
        return (part_a, part_b), (in_x(part_a), in_y(part_b))

    def spread_second(held, got):
        pair_a = jnp.stack([held[0], got[0]])
        pair_b = jnp.stack([held[1], got[1]])
        return (pair_a, pair_b), (in_y(pair_a), in_x(pair_b))

    def spread_rows(held, got):
        four_a = jnp.stack([held[0], got[0]])
        four_b = jnp.stack([held[1], got[1]], 1)
        four = jnp.concatenate([four_a, four_b], -1)
        return jnp.moveaxis(four, 2, 0).reshape(-1, half)

    def narrow(value):
        return value.astype(jnp.bfloat16)

    def widen(value):
        return value.astype(jnp.float32)

    gate_part, up_part, down_part = gate_weight[0], up_weight[0], down_weight[0]

    def gather_second(kept, got):
        pair_a, pair_b = kept[0] + widen(got[0]), kept[1] + widen(got[1])
        return (pair_a[0], pair_b[0]), (narrow(pair_a[1]), narrow(pair_b[1]))

    def gather_rows(kept, got):
        return jnp.concatenate([kept[0] + widen(got[0]), kept[1] + widen(got[1])], -1)

    def returned(sums, slots):
        return [
            (k, sums[at] if k == 0 else shift(narrow(sums[at]), -k))
            for at, k in enumerate(slots)
        ]

    early = [planes // 2]
    late = [k for k in range(1, planes) if k not in early]
    first_set, late_set = (0, 1 + len(early)), (0, len(late))
    join = lax.optimization_barrier

    def send_first(sent):
        return in_y(sent[0]), in_x(sent[1])

    def send_second(sent):
        return in_x(sent[0]), in_y(sent[1])

    slot_early = [shift(block, k) for k in early]
    held, got = spread_first([block])
    core, _ = join((core, block))
    core = hold(core)
    held, got, block, core = join((held, got, block, core))

    own, own_got = spread_second(held, got)
    entry_give = entry_half(core, gate_part, up_part)
    own, own_got, slot_early, block, entry_give = join(
        (own, own_got, slot_early, block, entry_give)
    )
    entry_other = in_core(entry_give)

    slot_late = [shift(block, k) for k in late]
    held, got = spread_first(slot_early)
    held, got = join((held, got))

    early_held, early_got = spread_second(held, got)
    down_give, down_own = exit_half(after(core, *held), down_part)
    early_held, early_got, slot_late, down_give, down_own = join(
        (early_held, early_got, slot_late, down_give, down_own)
    )

    down = (down_own, in_core(down_give))
    held, got = spread_first(slot_late)
    arrived = jnp.concatenate(
        [spread_rows(own, own_got), spread_rows(early_held, early_got)], 0
    )
    pre_other = entry(arrived, core, entry_other)
    held, got, pre_other, arrived = join((held, got, pre_other, arrived))

    late_held, late_got = spread_second(held, got)
    pre_own = entry(arrived, core, gate_part, up_part)
    inner = inner_units(pre_own, in_core(pre_other))
    inner = (inner, in_core(inner))
    (sent,) = exit_sums(inner, down, 2 * rows, [first_set], True)
    late_held, late_got, sent, inner = join((late_held, late_got, sent, inner))

    got = send_first(sent)
    arrived = spread_rows(late_held, late_got)
    pre_other = entry(arrived, core, entry_other)
    pre_own = entry(arrived, core, gate_part, up_part)
    (kept,) = exit_sums(inner, down, 2 * rows, [first_set], False)
    kept, got, pre_own, pre_other = join((kept, got, pre_own, pre_other))

    kept, sent = gather_second(kept, got)
    got = send_second(sent)
    inner = inner_units(pre_own, in_core(pre_other))
    inner = (inner, in_core(inner))
    (late_sent,) = exit_sums(inner, down, 2 * rows, [late_set], True)
    kept, got, inner, late_sent = join((kept, got, inner, late_sent))

    sums = gather_rows(kept, got)
    terms = returned(sums, [0] + early)
    late_got = send_first(late_sent)
    (late_kept,) = exit_sums(inner, down, 2 * rows, [late_set], False)
    attended = attend_more(0, None, *late_sent)
    late_kept, late_got, attended = join((late_kept, late_got, attended))

    late_kept, late_sent = gather_second(late_kept, late_got)
    late_got = send_second(late_sent)
    attended = attend_more(1, attended, *late_sent)
    late_kept, late_got, attended = join((late_kept, late_got, attended))

    terms += returned(gather_rows(late_kept, late_got), late)
    attended = attend_more(2, attended, *late_got)
    attended = attend_more(3, attended, attended)
    slots = [k for k, _ in terms]
    terms, attended = join(([term for _, term in terms], attended))
    terms = list(zip(slots, terms))
    total = 0.0
    for k, term in terms:
        total = total + mixing_of((plane + k) % planes) * widen(term)

    result = narrow(total)
    top, bottom = result[:rows], result[rows:]
    kept = jnp.where(first_core, top, bottom)
    got = in_core(jnp.where(first_core, bottom, top))
    routed = jnp.where(
        first_core, jnp.concatenate([kept, got], 1), jnp.concatenate([got, kept], 1)
    )
    return routed, attended


def solution(mesh):
    in_specs = (
        P(("groups", "expert"), None),
        P(("groups", "expert"), None),
        P(("groups", "expert"), None),
        P("expert", None, None),
        P("expert", None, None),
        P("expert", None, None),
        P(("groups", "expert"), None, None),
        P(("groups", "expert"), None, None),
        P(("groups", "expert")),
    )
    out_specs = (P(("groups", "expert"), None), P(("groups", "expert"), None, None))
    return jax.shard_map(
        on_device, mesh=mesh, in_specs=in_specs, out_specs=out_specs, check_vma=False
    )
```

```python
import functools
import math

import jax
import jax.numpy as jnp
from jax import lax
from jax.experimental import pallas as pl
from jax.experimental.pallas import tpu as pltpu
from jax.sharding import PartitionSpec as P

LAT = 512
SLICES = 8
AXIS = "expert"
ATTEND_CALLS = 4
ATTEND_TOGETHER = 4

score_scale = 0.07216878364870322

SMALL = pl.CostEstimate(flops=1, bytes_accessed=1, transcendentals=0)


def attend_kernel(lengths_ref, queries_ref, cache_ref, *refs, first):
    out_ref = refs[-1]
    each = out_ref.shape[0]
    masked = []
    for at in range(each):
        length = lengths_ref[first + pl.program_id(0) * each + at]
        scores = lax.dot_general(
            queries_ref[at],
            cache_ref[at],
            (((0,), (0,)), ((), ())),
            preferred_element_type=jnp.float32,
        )
        positions = lax.broadcasted_iota(jnp.int32, scores.shape, 1)
        masked.append(jnp.where(positions < length, scores * score_scale, -jnp.inf))
    weights = []
    for scores in masked:
        raised = jnp.exp(scores - jnp.max(scores, axis=-1, keepdims=True))
        weights.append((raised / jnp.sum(raised, axis=-1, keepdims=True)).astype(jnp.bfloat16))
    for at in range(each):
        out_ref[at] = lax.dot_general(
            weights[at],
            cache_ref[at, :LAT],
            (((1,), (1,)), ((), ())),
            preferred_element_type=jnp.float32,
        ).astype(jnp.bfloat16)


def attend(queries, latent_cache, lengths, first, count, held):
    requests, width, heads = queries.shape
    context = latent_cache.shape[2]
    aliases = {} if held is None else {3: 0}
    operands = (lengths, queries, latent_cache) + (() if held is None else (held,))
    each = math.gcd(count, ATTEND_TOGETHER)
    block = first // each
    return pl.pallas_call(
        functools.partial(attend_kernel, first=first),
        grid_spec=pltpu.PrefetchScalarGridSpec(
            num_scalar_prefetch=1,
            grid=(count // each,),
            in_specs=[
                pl.BlockSpec((each, width, heads), lambda i, _: (block + i, 0, 0)),
                pl.BlockSpec((each, width, context), lambda i, _: (block + i, 0, 0)),
            ]
            + ([] if held is None else [pl.BlockSpec(memory_space=pl.ANY)]),
            out_specs=pl.BlockSpec((each, heads, LAT), lambda i, _: (block + i, 0, 0)),
        ),
        out_shape=jax.ShapeDtypeStruct((requests, heads, LAT), jnp.bfloat16),
        input_output_aliases=aliases,
        compiler_params=pltpu.CompilerParams(vmem_limit_bytes=20 * 1024 * 1024),
        cost_estimate=SMALL,
        name="latent_attention",
    )(*operands)


def tile_of(half):
    return half // next(n for n in (7, 4, 2, 1) if half % (n * 128) == 0)


def entry_half_kernel(core_ref, gate_ref, up_ref, given_ref, kept_ref):
    half = kept_ref.shape[1]
    given = pl.multiple_of((1 - core_ref[0]) * half, half)
    kept = pl.multiple_of(core_ref[0] * half, half)
    for which, ref in enumerate((gate_ref, up_ref)):
        given_ref[which] = ref[pl.ds(given, half)]
        kept_ref[which] = ref[pl.ds(kept, half)]


def entry_half(core, gate, up):
    width, units = gate.shape
    shape = jax.ShapeDtypeStruct((2, width // 2, units), gate.dtype)
    return pl.pallas_call(
        entry_half_kernel,
        in_specs=[pl.BlockSpec(memory_space=pltpu.SMEM)]
        + [pl.BlockSpec(memory_space=pltpu.VMEM)] * 2,
        out_specs=[pl.BlockSpec(memory_space=pltpu.VMEM)] * 2,
        out_shape=[shape, shape],
        compiler_params=pltpu.CompilerParams(vmem_limit_bytes=16 * 1024 * 1024),
        cost_estimate=SMALL,
        name="entry_half",
    )(core.reshape(1), gate, up)


def hold_kernel(in_ref, out_ref):
    out_ref[0] = in_ref[0]


def hold(value):
    return pl.pallas_call(
        hold_kernel,
        in_specs=[pl.BlockSpec(memory_space=pltpu.SMEM)],
        out_specs=pl.BlockSpec(memory_space=pltpu.SMEM),
        out_shape=jax.ShapeDtypeStruct((1,), value.dtype),
        compiler_params=pltpu.CompilerParams(vmem_limit_bytes=1024 * 1024),
        cost_estimate=SMALL,
        name="hold",
    )(value.reshape(1))[0]


def exit_half_kernel(_, given_ref, kept_ref, given_out_ref, kept_out_ref):
    given_out_ref[...] = given_ref[...]
    kept_out_ref[...] = kept_ref[...]


def exit_half(core, down):
    units, width = down.shape
    tile = tile_of(width // 2)
    steps = width // 2 // tile
    shape = jax.ShapeDtypeStruct((units, width // 2), down.dtype)
    return pl.pallas_call(
        exit_half_kernel,
        grid_spec=pltpu.PrefetchScalarGridSpec(
            num_scalar_prefetch=1,
            grid=(steps,),
            in_specs=[
                pl.BlockSpec((units, tile), lambda i, core: (0, (1 - core[0]) * steps + i)),
                pl.BlockSpec((units, tile), lambda i, core: (0, core[0] * steps + i)),
            ],
            out_specs=[pl.BlockSpec((units, tile), lambda i, core: (0, i))] * 2,
        ),
        out_shape=[shape, shape],
        compiler_params=pltpu.CompilerParams(vmem_limit_bytes=16 * 1024 * 1024),
        cost_estimate=SMALL,
        name="exit_half",
    )(core.reshape(1), down, down)


def entry_kernel(rows_ref, weight_ref, out_ref):
    for which in range(2):
        out_ref[which] = jnp.dot(
            rows_ref[...], weight_ref[which], preferred_element_type=jnp.float32
        )


def entry(rows, weight):
    return pl.pallas_call(
        entry_kernel,
        in_specs=[pl.BlockSpec(memory_space=pltpu.VMEM)] * 2,
        out_specs=pl.BlockSpec(memory_space=pltpu.VMEM),
        out_shape=jax.ShapeDtypeStruct((2, rows.shape[0], weight.shape[2]), jnp.float32),
        compiler_params=pltpu.CompilerParams(vmem_limit_bytes=16 * 1024 * 1024),
        cost_estimate=SMALL,
        name="entry_products",
    )(rows, weight)


def inner_kernel(own_ref, other_ref, out_ref):
    gate_value = own_ref[0] + other_ref[0]
    up_value = own_ref[1] + other_ref[1]
    silu = gate_value / (1.0 + jnp.exp(-gate_value))
    out_ref[...] = (silu * up_value).astype(out_ref.dtype)


def inner_units(own, other, vmem=12):
    return pl.pallas_call(
        inner_kernel,
        in_specs=[pl.BlockSpec(memory_space=pltpu.VMEM)] * 2,
        out_specs=pl.BlockSpec(memory_space=pltpu.VMEM),
        out_shape=jax.ShapeDtypeStruct(own.shape[1:], jnp.bfloat16),
        compiler_params=pltpu.CompilerParams(vmem_limit_bytes=vmem * 1024 * 1024),
        cost_estimate=SMALL,
        name="inner_units",
    )(own, other)


def exit_kernel(own_ref, other_ref, down_own_ref, down_other_ref, *out_refs, sets, rows, sent):
    quarter = down_own_ref.shape[1] // 2
    tile = math.gcd(quarter, 256)

    def picked(ref, second):
        strips = []
        for begin, slots in sets:
            for slot in range(slots):
                for other in range(2):
                    y, x = (other, sent) if second else (sent, other)
                    at = ((begin + slot) * 4 + y * 2 + x) * rows
                    strips.append(ref[at : at + rows])
        return jnp.concatenate(strips, 0)

    for second in range(2):
        own, other = picked(own_ref, second), picked(other_ref, second)
        for at in range(quarter // tile):
            source = slice(second * quarter + at * tile, second * quarter + (at + 1) * tile)
            columns = slice(at * tile, (at + 1) * tile)
            part = jnp.dot(own, down_own_ref[:, source], preferred_element_type=jnp.float32)
            part += jnp.dot(other, down_other_ref[:, source], preferred_element_type=jnp.float32)
            row = 0
            for number, (_, slots) in enumerate(sets):
                target = out_refs[2 * number + second]
                for slot in range(slots):
                    for which in range(2):
                        value = part[row : row + rows]
                        target[which, slot, :, columns] = value.astype(target.dtype)
                        row += rows


def exit_sums(inner, down, rows, sets, sent):
    quarter = down[0].shape[1] // 2
    dtype = jnp.bfloat16 if sent else jnp.float32
    shapes = []
    for _, slots in sets:
        shapes += [jax.ShapeDtypeStruct((2, slots, rows, quarter), dtype)] * 2
    outs = pl.pallas_call(
        functools.partial(exit_kernel, sets=sets, rows=rows, sent=int(sent)),
        in_specs=[pl.BlockSpec(memory_space=pltpu.VMEM)] * 4,
        out_specs=[pl.BlockSpec(memory_space=pltpu.VMEM)] * len(shapes),
        out_shape=shapes,
        compiler_params=pltpu.CompilerParams(vmem_limit_bytes=16 * 1024 * 1024),
        cost_estimate=SMALL,
        name="exit_sums",
    )(*inner, *down)
    return [tuple(outs[at : at + 2]) for at in range(0, len(outs), 2)]


def after(value, *others):
    return lax.optimization_barrier((value,) + others)[0]


def on_device(
    hidden,
    expert_ids,
    route_weights,
    gate_weight,
    up_weight,
    down_weight,
    queries,
    latent_cache,
    lengths,
):
    devices = lax.axis_size(AXIS)
    planes = devices // SLICES
    me = lax.axis_index(AXIS)
    core, plane = lax.rem(me, 2), lax.div(me, SLICES)
    rows, width = hidden.shape
    half, quarter = width // 2, width // 4
    first_core = core == 0

    def swap(value, bit):
        return lax.ppermute(value, AXIS, [(i, i ^ bit) for i in range(devices)])

    def shift(value, by):
        return lax.ppermute(
            value, AXIS, [(i, (i + SLICES * by) % devices) for i in range(devices)]
        )

    in_core = functools.partial(swap, bit=1)
    in_x = functools.partial(swap, bit=2)
    in_y = functools.partial(swap, bit=4)

    low, high = hidden[:, :half], hidden[:, half:]
    kept = jnp.where(first_core, low, high)
    got = in_core(jnp.where(first_core, high, low))
    block = jnp.where(
        first_core, jnp.concatenate([kept, got], 0), jnp.concatenate([got, kept], 0)
    )
    choose = (
        expert_ids[:, :, None] == jnp.arange(planes, dtype=jnp.int32)[None, None, :]
    ).astype(jnp.float32)
    mixing = jnp.sum(route_weights[:, :, None] * choose, axis=1)
    mixing_other = in_core(mixing)
    mixing = jnp.where(
        first_core,
        jnp.concatenate([mixing, mixing_other], 0),
        jnp.concatenate([mixing_other, mixing], 0),
    )

    def mixing_of(expert):
        pick = jnp.arange(planes)[None, :] == expert
        return jnp.sum(jnp.where(pick, mixing, 0.0), axis=1, keepdims=True)

    queries_turned = jnp.swapaxes(queries, 1, 2)
    cache_turned = jnp.swapaxes(latent_cache, 1, 2)
    step = rows // ATTEND_CALLS

    def attend_more(number, held, *others):
        return attend(
            queries_turned, cache_turned, after(lengths, *others), number * step, step, held
        )

    def spread_first(slots):
        part_a = jnp.stack([slot[:, :quarter] for slot in slots])
        part_b = jnp.stack([slot[:, quarter:] for slot in slots])
        return (part_a, part_b), (in_x(part_a), in_y(part_b))

    def spread_second(held, got):
        pair_a = jnp.stack([held[0], got[0]])
        pair_b = jnp.stack([held[1], got[1]])
        return (pair_a, pair_b), (in_y(pair_a), in_x(pair_b))

    def spread_rows(held, got):
        four_a = jnp.stack([held[0], got[0]])
        four_b = jnp.stack([held[1], got[1]], 1)
        four = jnp.concatenate([four_a, four_b], -1)
        return jnp.moveaxis(four, 2, 0).reshape(-1, half)

    def narrow(value):
        return value.astype(jnp.bfloat16)

    def widen(value):
        return value.astype(jnp.float32)

    gate_part, up_part, down_part = gate_weight[0], up_weight[0], down_weight[0]

    def gather_second(kept, got):
        pair_a, pair_b = kept[0] + widen(got[0]), kept[1] + widen(got[1])
        return (pair_a[0], pair_b[0]), (narrow(pair_a[1]), narrow(pair_b[1]))

    def gather_rows(kept, got):
        return jnp.concatenate([kept[0] + widen(got[0]), kept[1] + widen(got[1])], -1)

    def returned(sums, slots):
        return [
            (k, sums[at] if k == 0 else shift(narrow(sums[at]), -k))
            for at, k in enumerate(slots)
        ]

    early = [1, planes - 1]
    late = list(range(2, planes - 1))
    own_set, early_set, late_set = (0, 1), (1, len(early)), (0, len(late))
    join = lax.optimization_barrier

    def send_first(sent):
        return in_y(sent[0]), in_x(sent[1])

    def send_second(sent):
        return in_x(sent[0]), in_y(sent[1])

    slot_early = [shift(block, k) for k in early]
    held, got = spread_first([block])
    core, _ = join((core, block))
    core = hold(core)
    held, got, block, core = join((held, got, block, core))

    own, own_got = spread_second(held, got)
    entry_give, entry_own = entry_half(core, gate_part, up_part)
    own, own_got, slot_early, block, entry_give, entry_own = join(
        (own, own_got, slot_early, block, entry_give, entry_own)
    )
    entry_other = in_core(entry_give)

    slot_late = [shift(block, k) for k in late]
    held, got = spread_first(slot_early)
    shares = [mixing_of(lax.rem(plane + k, planes)) for k in range(planes)]
    held, got, shares = join((held, got, shares))

    early_held, early_got = spread_second(held, got)
    down_give, down_own = exit_half(after(core, *held), down_part)
    held, got = spread_first(slot_late)
    early_held, early_got, held, got, down_give, down_own = join(
        (early_held, early_got, held, got, down_give, down_own)
    )

    down = (down_own, in_core(down_give))
    arrived = jnp.concatenate(
        [spread_rows(own, own_got), spread_rows(early_held, early_got)], 0
    )
    pre_other = entry(arrived, entry_other)
    late_held, late_got = spread_second(held, got)
    pre_own = entry(arrived, entry_own)
    inner = inner_units(pre_own, in_core(pre_other))
    inner = (inner, in_core(inner))
    (sent,) = exit_sums(inner, down, 2 * rows, [early_set], True)
    late_held, late_got, sent, inner = join((late_held, late_got, sent, inner))

    got = send_first(sent)
    arrived = spread_rows(late_held, late_got)
    pre_other = entry(arrived, entry_other)
    pre_own = entry(arrived, entry_own)
    (kept,) = exit_sums(inner, down, 2 * rows, [early_set], False)
    (own_sent,) = exit_sums(inner, down, 2 * rows, [own_set], True)
    (own_kept,) = exit_sums(inner, down, 2 * rows, [own_set], False)
    attended = attend_more(0, None, *sent)
    kept, got, own_sent, own_kept, pre_own, pre_other, attended = join(
        (kept, got, own_sent, own_kept, pre_own, pre_other, attended)
    )

    kept, sent = gather_second(kept, got)
    got = send_second(sent)
    inner = inner_units(pre_own, in_core(pre_other))
    inner = (inner, in_core(inner))
    (late_sent,) = exit_sums(inner, down, 2 * rows, [late_set], True)
    (late_kept,) = exit_sums(inner, down, 2 * rows, [late_set], False)
    kept, got, late_sent, late_kept = join((kept, got, late_sent, late_kept))

    terms = returned(gather_rows(kept, got), early)
    got = send_first(late_sent)
    attended = attend_more(1, attended, *late_sent)
    late_kept, got, attended = join((late_kept, got, attended))

    kept, sent = gather_second(late_kept, got)
    got = send_second(sent)
    attended = attend_more(2, attended, *sent)
    kept, got, attended, own_sent = join((kept, got, attended, own_sent))

    terms += returned(gather_rows(kept, got), late)
    got = send_first(own_sent)
    attended = attend_more(3, attended, *own_sent)
    own_kept, got, attended = join((own_kept, got, attended))

    kept, sent = gather_second(own_kept, got)
    got = send_second(sent)
    terms += returned(gather_rows(kept, got), [0])
    slots = [k for k, _ in terms]
    terms, attended = join(([term for _, term in terms], attended))
    terms = list(zip(slots, terms))
    total = 0.0
    for k, term in terms:
        total = total + shares[k] * widen(term)

    result = narrow(total)
    top, bottom = result[:rows], result[rows:]
    kept = jnp.where(first_core, top, bottom)
    got = in_core(jnp.where(first_core, bottom, top))
    routed = jnp.where(
        first_core, jnp.concatenate([kept, got], 1), jnp.concatenate([got, kept], 1)
    )
    return routed, attended


def solution(mesh):
    in_specs = (
        P(("groups", "expert"), None),
        P(("groups", "expert"), None),
        P(("groups", "expert"), None),
        P("expert", None, None),
        P("expert", None, None),
        P("expert", None, None),
        P(("groups", "expert"), None, None),
        P(("groups", "expert"), None, None),
        P(("groups", "expert")),
    )
    out_specs = (P(("groups", "expert"), None), P(("groups", "expert"), None, None))
    return jax.shard_map(
        on_device, mesh=mesh, in_specs=in_specs, out_specs=out_specs, check_vma=False
    )
```

```python
import functools
import math

import jax
import jax.numpy as jnp
from jax import lax
from jax.experimental import pallas as pl
from jax.experimental.pallas import tpu as pltpu
from jax.sharding import PartitionSpec as P

LAT = 512
SLICES = 8
AXIS = "expert"
ATTEND_CALLS = 4
ATTEND_TOGETHER = 4

score_scale = 0.07216878364870322

SMALL = pl.CostEstimate(flops=1, bytes_accessed=1, transcendentals=0)


def attend_kernel(lengths_ref, queries_ref, cache_ref, *refs, first):
    out_ref = refs[-1]
    each = out_ref.shape[0]
    masked = []
    for at in range(each):
        length = lengths_ref[first + pl.program_id(0) * each + at]
        scores = lax.dot_general(
            queries_ref[at],
            cache_ref[at],
            (((0,), (0,)), ((), ())),
            preferred_element_type=jnp.float32,
        )
        positions = lax.broadcasted_iota(jnp.int32, scores.shape, 1)
        masked.append(jnp.where(positions < length, scores * score_scale, -jnp.inf))
    weights = []
    for scores in masked:
        raised = jnp.exp(scores - jnp.max(scores, axis=-1, keepdims=True))
        weights.append((raised / jnp.sum(raised, axis=-1, keepdims=True)).astype(jnp.bfloat16))
    for at in range(each):
        out_ref[at] = lax.dot_general(
            weights[at],
            cache_ref[at, :LAT],
            (((1,), (1,)), ((), ())),
            preferred_element_type=jnp.float32,
        ).astype(jnp.bfloat16)


def attend(queries, latent_cache, lengths, first, count, held):
    requests, width, heads = queries.shape
    context = latent_cache.shape[2]
    aliases = {} if held is None else {3: 0}
    operands = (lengths, queries, latent_cache) + (() if held is None else (held,))
    each = math.gcd(count, ATTEND_TOGETHER)
    block = first // each
    return pl.pallas_call(
        functools.partial(attend_kernel, first=first),
        grid_spec=pltpu.PrefetchScalarGridSpec(
            num_scalar_prefetch=1,
            grid=(count // each,),
            in_specs=[
                pl.BlockSpec((each, width, heads), lambda i, _: (block + i, 0, 0)),
                pl.BlockSpec((each, width, context), lambda i, _: (block + i, 0, 0)),
            ]
            + ([] if held is None else [pl.BlockSpec(memory_space=pl.ANY)]),
            out_specs=pl.BlockSpec((each, heads, LAT), lambda i, _: (block + i, 0, 0)),
        ),
        out_shape=jax.ShapeDtypeStruct((requests, heads, LAT), jnp.bfloat16),
        input_output_aliases=aliases,
        compiler_params=pltpu.CompilerParams(vmem_limit_bytes=20 * 1024 * 1024),
        cost_estimate=SMALL,
        name="latent_attention",
    )(*operands)


def tile_of(half):
    return half // next(n for n in (7, 4, 2, 1) if half % (n * 128) == 0)


def entry_half_kernel(core_ref, gate_ref, up_ref, given_ref, kept_ref):
    half = kept_ref.shape[1]
    given = pl.multiple_of((1 - core_ref[0]) * half, half)
    kept = pl.multiple_of(core_ref[0] * half, half)
    for which, ref in enumerate((gate_ref, up_ref)):
        given_ref[which] = ref[pl.ds(given, half)]
        kept_ref[which] = ref[pl.ds(kept, half)]


def entry_half(core, gate, up):
    width, units = gate.shape
    shape = jax.ShapeDtypeStruct((2, width // 2, units), gate.dtype)
    return pl.pallas_call(
        entry_half_kernel,
        in_specs=[pl.BlockSpec(memory_space=pltpu.SMEM)]
        + [pl.BlockSpec(memory_space=pltpu.VMEM)] * 2,
        out_specs=[pl.BlockSpec(memory_space=pltpu.VMEM)] * 2,
        out_shape=[shape, shape],
        compiler_params=pltpu.CompilerParams(vmem_limit_bytes=16 * 1024 * 1024),
        cost_estimate=SMALL,
        name="entry_half",
    )(core.reshape(1), gate, up)


def hold_kernel(in_ref, out_ref):
    out_ref[0] = in_ref[0]


def hold(value):
    return pl.pallas_call(
        hold_kernel,
        in_specs=[pl.BlockSpec(memory_space=pltpu.SMEM)],
        out_specs=pl.BlockSpec(memory_space=pltpu.SMEM),
        out_shape=jax.ShapeDtypeStruct((1,), value.dtype),
        compiler_params=pltpu.CompilerParams(vmem_limit_bytes=1024 * 1024),
        cost_estimate=SMALL,
        name="hold",
    )(value.reshape(1))[0]


def exit_half_kernel(_, given_ref, kept_ref, given_out_ref, kept_out_ref):
    given_out_ref[...] = given_ref[...]
    kept_out_ref[...] = kept_ref[...]


def exit_half(core, down):
    units, width = down.shape
    tile = tile_of(width // 2)
    steps = width // 2 // tile
    shape = jax.ShapeDtypeStruct((units, width // 2), down.dtype)
    return pl.pallas_call(
        exit_half_kernel,
        grid_spec=pltpu.PrefetchScalarGridSpec(
            num_scalar_prefetch=1,
            grid=(steps,),
            in_specs=[
                pl.BlockSpec((units, tile), lambda i, core: (0, (1 - core[0]) * steps + i)),
                pl.BlockSpec((units, tile), lambda i, core: (0, core[0] * steps + i)),
            ],
            out_specs=[pl.BlockSpec((units, tile), lambda i, core: (0, i))] * 2,
        ),
        out_shape=[shape, shape],
        compiler_params=pltpu.CompilerParams(vmem_limit_bytes=16 * 1024 * 1024),
        cost_estimate=SMALL,
        name="exit_half",
    )(core.reshape(1), down, down)


def entry_kernel(rows_ref, weight_ref, out_ref):
    for which in range(2):
        out_ref[which] = jnp.dot(
            rows_ref[...], weight_ref[which], preferred_element_type=jnp.float32
        )


def entry(rows, weight):
    return pl.pallas_call(
        entry_kernel,
        in_specs=[pl.BlockSpec(memory_space=pltpu.VMEM)] * 2,
        out_specs=pl.BlockSpec(memory_space=pltpu.VMEM),
        out_shape=jax.ShapeDtypeStruct((2, rows.shape[0], weight.shape[2]), jnp.float32),
        compiler_params=pltpu.CompilerParams(vmem_limit_bytes=16 * 1024 * 1024),
        cost_estimate=SMALL,
        name="entry_products",
    )(rows, weight)


def inner_kernel(own_ref, other_ref, out_ref):
    gate_value = own_ref[0] + other_ref[0]
    up_value = own_ref[1] + other_ref[1]
    silu = gate_value / (1.0 + jnp.exp(-gate_value))
    out_ref[...] = (silu * up_value).astype(out_ref.dtype)


def inner_units(own, other, vmem=12):
    return pl.pallas_call(
        inner_kernel,
        in_specs=[pl.BlockSpec(memory_space=pltpu.VMEM)] * 2,
        out_specs=pl.BlockSpec(memory_space=pltpu.VMEM),
        out_shape=jax.ShapeDtypeStruct(own.shape[1:], jnp.bfloat16),
        compiler_params=pltpu.CompilerParams(vmem_limit_bytes=vmem * 1024 * 1024),
        cost_estimate=SMALL,
        name="inner_units",
    )(own, other)


def exit_kernel(own_ref, other_ref, down_own_ref, down_other_ref, *out_refs, sets, rows, sent):
    quarter = down_own_ref.shape[1] // 2
    tile = math.gcd(quarter, 256)

    def picked(ref, second):
        strips = []
        for begin, slots in sets:
            for slot in range(slots):
                for other in range(2):
                    y, x = (other, sent) if second else (sent, other)
                    at = ((begin + slot) * 4 + y * 2 + x) * rows
                    strips.append(ref[at : at + rows])
        return jnp.concatenate(strips, 0)

    for second in range(2):
        own, other = picked(own_ref, second), picked(other_ref, second)
        for at in range(quarter // tile):
            source = slice(second * quarter + at * tile, second * quarter + (at + 1) * tile)
            columns = slice(at * tile, (at + 1) * tile)
            part = jnp.dot(own, down_own_ref[:, source], preferred_element_type=jnp.float32)
            part += jnp.dot(other, down_other_ref[:, source], preferred_element_type=jnp.float32)
            row = 0
            for number, (_, slots) in enumerate(sets):
                target = out_refs[2 * number + second]
                for slot in range(slots):
                    for which in range(2):
                        value = part[row : row + rows]
                        target[which, slot, :, columns] = value.astype(target.dtype)
                        row += rows


def exit_sums(inner, down, rows, sets, sent):
    quarter = down[0].shape[1] // 2
    dtype = jnp.bfloat16 if sent else jnp.float32
    shapes = []
    for _, slots in sets:
        shapes += [jax.ShapeDtypeStruct((2, slots, rows, quarter), dtype)] * 2
    outs = pl.pallas_call(
        functools.partial(exit_kernel, sets=sets, rows=rows, sent=int(sent)),
        in_specs=[pl.BlockSpec(memory_space=pltpu.VMEM)] * 4,
        out_specs=[pl.BlockSpec(memory_space=pltpu.VMEM)] * len(shapes),
        out_shape=shapes,
        compiler_params=pltpu.CompilerParams(vmem_limit_bytes=16 * 1024 * 1024),
        cost_estimate=SMALL,
        name="exit_sums",
    )(*inner, *down)
    return [tuple(outs[at : at + 2]) for at in range(0, len(outs), 2)]


def after(value, *others):
    return lax.optimization_barrier((value,) + others)[0]


def on_device(
    hidden,
    expert_ids,
    route_weights,
    gate_weight,
    up_weight,
    down_weight,
    queries,
    latent_cache,
    lengths,
):
    devices = lax.axis_size(AXIS)
    planes = devices // SLICES
    me = lax.axis_index(AXIS)
    core, plane = lax.rem(me, 2), lax.div(me, SLICES)
    rows, width = hidden.shape
    half, quarter = width // 2, width // 4
    first_core = core == 0

    def swap(value, bit):
        return lax.ppermute(value, AXIS, [(i, i ^ bit) for i in range(devices)])

    def shift(value, by):
        return lax.ppermute(
            value, AXIS, [(i, (i + SLICES * by) % devices) for i in range(devices)]
        )

    in_core = functools.partial(swap, bit=1)
    in_x = functools.partial(swap, bit=2)
    in_y = functools.partial(swap, bit=4)

    low, high = hidden[:, :half], hidden[:, half:]
    kept = jnp.where(first_core, low, high)
    got = in_core(jnp.where(first_core, high, low))
    block = jnp.where(
        first_core, jnp.concatenate([kept, got], 0), jnp.concatenate([got, kept], 0)
    )
    choose = (
        expert_ids[:, :, None] == jnp.arange(planes, dtype=jnp.int32)[None, None, :]
    ).astype(jnp.float32)
    mixing = jnp.sum(route_weights[:, :, None] * choose, axis=1)
    mixing_other = in_core(mixing)
    mixing = jnp.where(
        first_core,
        jnp.concatenate([mixing, mixing_other], 0),
        jnp.concatenate([mixing_other, mixing], 0),
    )

    def mixing_of(expert):
        pick = jnp.arange(planes)[None, :] == expert
        return jnp.sum(jnp.where(pick, mixing, 0.0), axis=1, keepdims=True)

    queries_turned = jnp.swapaxes(queries, 1, 2)
    cache_turned = jnp.swapaxes(latent_cache, 1, 2)
    step = rows // ATTEND_CALLS

    def attend_more(number, held, *others):
        return attend(
            queries_turned, cache_turned, after(lengths, *others), number * step, step, held
        )

    def spread_first(slots):
        part_a = jnp.stack([slot[:, :quarter] for slot in slots])
        part_b = jnp.stack([slot[:, quarter:] for slot in slots])
        return (part_a, part_b), (in_x(part_a), in_y(part_b))

    def spread_second(held, got):
        pair_a = jnp.stack([held[0], got[0]])
        pair_b = jnp.stack([held[1], got[1]])
        return (pair_a, pair_b), (in_y(pair_a), in_x(pair_b))

    def spread_rows(held, got):
        four_a = jnp.stack([held[0], got[0]])
        four_b = jnp.stack([held[1], got[1]], 1)
        four = jnp.concatenate([four_a, four_b], -1)
        return jnp.moveaxis(four, 2, 0).reshape(-1, half)

    def narrow(value):
        return value.astype(jnp.bfloat16)

    def widen(value):
        return value.astype(jnp.float32)

    gate_part, up_part, down_part = gate_weight[0], up_weight[0], down_weight[0]

    def gather_second(kept, got):
        pair_a, pair_b = kept[0] + widen(got[0]), kept[1] + widen(got[1])
        return (pair_a[0], pair_b[0]), (narrow(pair_a[1]), narrow(pair_b[1]))

    def gather_rows(kept, got):
        return jnp.concatenate([kept[0] + widen(got[0]), kept[1] + widen(got[1])], -1)

    def returned(sums, slots):
        return [
            (k, sums[at] if k == 0 else shift(narrow(sums[at]), -k))
            for at, k in enumerate(slots)
        ]

    early = [1, planes - 1]
    late = list(range(2, planes - 1))
    own_set, early_set, late_set = (0, 1), (1, len(early)), (0, len(late))
    join = lax.optimization_barrier

    def send_first(sent):
        return in_y(sent[0]), in_x(sent[1])

    def send_second(sent):
        return in_x(sent[0]), in_y(sent[1])

    slot_early = [shift(block, k) for k in early]
    held, got = spread_first([block])
    core, _ = join((core, block))
    core = hold(core)
    held, got, block, core = join((held, got, block, core))

    own, own_got = spread_second(held, got)
    entry_give, entry_own = entry_half(core, gate_part, up_part)
    own, own_got, slot_early, block, entry_give, entry_own = join(
        (own, own_got, slot_early, block, entry_give, entry_own)
    )
    entry_other = in_core(entry_give)

    slot_late = [shift(block, k) for k in late]
    held, got = spread_first(slot_early)
    shares = [mixing_of(lax.rem(plane + k, planes)) for k in range(planes)]
    held, got, shares = join((held, got, shares))

    early_held, early_got = spread_second(held, got)
    down_give, down_own = exit_half(after(core, *held), down_part)
    held, got = spread_first(slot_late)
    early_held, early_got, held, got, down_give, down_own = join(
        (early_held, early_got, held, got, down_give, down_own)
    )

    down = (down_own, in_core(down_give))
    arrived = jnp.concatenate(
        [spread_rows(own, own_got), spread_rows(early_held, early_got)], 0
    )
    pre_other = entry(arrived, entry_other)
    late_held, late_got = spread_second(held, got)
    pre_own = entry(arrived, entry_own)
    inner = inner_units(pre_own, in_core(pre_other))
    inner = (inner, in_core(inner))
    (sent,) = exit_sums(inner, down, 2 * rows, [early_set], True)
    late_held, late_got, sent, inner = join((late_held, late_got, sent, inner))

    got = send_first(sent)
    arrived = spread_rows(late_held, late_got)
    pre_other = entry(arrived, entry_other)
    pre_own = entry(arrived, entry_own)
    (kept,) = exit_sums(inner, down, 2 * rows, [early_set], False)
    (own_sent,) = exit_sums(inner, down, 2 * rows, [own_set], True)
    (own_kept,) = exit_sums(inner, down, 2 * rows, [own_set], False)
    attended = attend_more(0, None, *sent)
    kept, got, own_sent, own_kept, pre_own, pre_other, attended = join(
        (kept, got, own_sent, own_kept, pre_own, pre_other, attended)
    )

    kept, sent = gather_second(kept, got)
    got = send_second(sent)
    inner = inner_units(pre_own, in_core(pre_other))
    inner = (inner, in_core(inner))
    (late_sent,) = exit_sums(inner, down, 2 * rows, [late_set], True)
    (late_kept,) = exit_sums(inner, down, 2 * rows, [late_set], False)
    kept, got, late_sent, late_kept = join((kept, got, late_sent, late_kept))

    terms = returned(gather_rows(kept, got), early)
    got = send_first(late_sent)
    attended = attend_more(1, attended, *late_sent)
    late_kept, got, attended, own_sent = join((late_kept, got, attended, own_sent))

    kept, sent = gather_second(late_kept, got)
    got = send_second(sent)
    attended = attend_more(2, attended, *sent)
    kept, got, attended = join((kept, got, attended))

    terms += returned(gather_rows(kept, got), late)
    got = send_first(own_sent)
    attended = attend_more(3, attended, *kept)
    own_kept, got, attended = join((own_kept, got, attended))

    kept, sent = gather_second(own_kept, got)
    got = send_second(sent)
    terms += returned(gather_rows(kept, got), [0])
    slots = [k for k, _ in terms]
    terms, attended = join(([term for _, term in terms], attended))
    terms = list(zip(slots, terms))
    total = 0.0
    for k, term in terms:
        total = total + shares[k] * widen(term)

    result = narrow(total)
    top, bottom = result[:rows], result[rows:]
    kept = jnp.where(first_core, top, bottom)
    got = in_core(jnp.where(first_core, bottom, top))
    routed = jnp.where(
        first_core, jnp.concatenate([kept, got], 1), jnp.concatenate([got, kept], 1)
    )
    return routed, attended


def solution(mesh):
    in_specs = (
        P(("groups", "expert"), None),
        P(("groups", "expert"), None),
        P(("groups", "expert"), None),
        P("expert", None, None),
        P("expert", None, None),
        P("expert", None, None),
        P(("groups", "expert"), None, None),
        P(("groups", "expert"), None, None),
        P(("groups", "expert")),
    )
    out_specs = (P(("groups", "expert"), None), P(("groups", "expert"), None, None))
    return jax.shard_map(
        on_device, mesh=mesh, in_specs=in_specs, out_specs=out_specs, check_vma=False
    )
```

```python
import functools
import math

import jax
import jax.numpy as jnp
from jax import lax
from jax.experimental import pallas as pl
from jax.experimental.pallas import tpu as pltpu
from jax.sharding import PartitionSpec as P

LAT = 512
SLICES = 8
AXIS = "expert"
ATTEND_CALLS = 4
ATTEND_TOGETHER = 4

score_scale = 0.07216878364870322

SMALL = pl.CostEstimate(flops=1, bytes_accessed=1, transcendentals=0)


def attend_kernel(lengths_ref, queries_ref, cache_ref, *refs, first):
    out_ref = refs[-1]
    each = out_ref.shape[0]
    masked = []
    for at in range(each):
        length = lengths_ref[first + pl.program_id(0) * each + at]
        scores = lax.dot_general(
            queries_ref[at],
            cache_ref[at],
            (((0,), (0,)), ((), ())),
            preferred_element_type=jnp.float32,
        )
        positions = lax.broadcasted_iota(jnp.int32, scores.shape, 1)
        masked.append(jnp.where(positions < length, scores * score_scale, -jnp.inf))
    weights = []
    for scores in masked:
        raised = jnp.exp(scores - jnp.max(scores, axis=-1, keepdims=True))
        weights.append((raised / jnp.sum(raised, axis=-1, keepdims=True)).astype(jnp.bfloat16))
    for at in range(each):
        out_ref[at] = lax.dot_general(
            weights[at],
            cache_ref[at, :LAT],
            (((1,), (1,)), ((), ())),
            preferred_element_type=jnp.float32,
        ).astype(jnp.bfloat16)


def attend(queries, latent_cache, lengths, first, count, held):
    requests, width, heads = queries.shape
    context = latent_cache.shape[2]
    aliases = {} if held is None else {3: 0}
    operands = (lengths, queries, latent_cache) + (() if held is None else (held,))
    each = math.gcd(count, ATTEND_TOGETHER)
    block = first // each
    return pl.pallas_call(
        functools.partial(attend_kernel, first=first),
        grid_spec=pltpu.PrefetchScalarGridSpec(
            num_scalar_prefetch=1,
            grid=(count // each,),
            in_specs=[
                pl.BlockSpec((each, width, heads), lambda i, _: (block + i, 0, 0)),
                pl.BlockSpec((each, width, context), lambda i, _: (block + i, 0, 0)),
            ]
            + ([] if held is None else [pl.BlockSpec(memory_space=pl.ANY)]),
            out_specs=pl.BlockSpec((each, heads, LAT), lambda i, _: (block + i, 0, 0)),
        ),
        out_shape=jax.ShapeDtypeStruct((requests, heads, LAT), jnp.bfloat16),
        input_output_aliases=aliases,
        compiler_params=pltpu.CompilerParams(vmem_limit_bytes=20 * 1024 * 1024),
        cost_estimate=SMALL,
        name="latent_attention",
    )(*operands)


def tile_of(half):
    return half // next(n for n in (7, 4, 2, 1) if half % (n * 128) == 0)


def entry_half_kernel(core_ref, gate_ref, up_ref, given_ref, kept_ref):
    half = kept_ref.shape[1]
    given = pl.multiple_of((1 - core_ref[0]) * half, half)
    kept = pl.multiple_of(core_ref[0] * half, half)
    for which, ref in enumerate((gate_ref, up_ref)):
        given_ref[which] = ref[pl.ds(given, half)]
        kept_ref[which] = ref[pl.ds(kept, half)]


def entry_half(core, gate, up):
    width, units = gate.shape
    shape = jax.ShapeDtypeStruct((2, width // 2, units), gate.dtype)
    return pl.pallas_call(
        entry_half_kernel,
        in_specs=[pl.BlockSpec(memory_space=pltpu.SMEM)]
        + [pl.BlockSpec(memory_space=pltpu.VMEM)] * 2,
        out_specs=[pl.BlockSpec(memory_space=pltpu.VMEM)] * 2,
        out_shape=[shape, shape],
        compiler_params=pltpu.CompilerParams(vmem_limit_bytes=16 * 1024 * 1024),
        cost_estimate=SMALL,
        name="entry_half",
    )(core.reshape(1), gate, up)


def hold_kernel(in_ref, out_ref):
    out_ref[0] = in_ref[0]


def hold(value):
    return pl.pallas_call(
        hold_kernel,
        in_specs=[pl.BlockSpec(memory_space=pltpu.SMEM)],
        out_specs=pl.BlockSpec(memory_space=pltpu.SMEM),
        out_shape=jax.ShapeDtypeStruct((1,), value.dtype),
        compiler_params=pltpu.CompilerParams(vmem_limit_bytes=1024 * 1024),
        cost_estimate=SMALL,
        name="hold",
    )(value.reshape(1))[0]


def exit_half_kernel(_, given_ref, kept_ref, given_out_ref, kept_out_ref):
    given_out_ref[...] = given_ref[...]
    kept_out_ref[...] = kept_ref[...]


def exit_half(core, down):
    units, width = down.shape
    tile = tile_of(width // 2)
    steps = width // 2 // tile
    shape = jax.ShapeDtypeStruct((units, width // 2), down.dtype)
    return pl.pallas_call(
        exit_half_kernel,
        grid_spec=pltpu.PrefetchScalarGridSpec(
            num_scalar_prefetch=1,
            grid=(steps,),
            in_specs=[
                pl.BlockSpec((units, tile), lambda i, core: (0, (1 - core[0]) * steps + i)),
                pl.BlockSpec((units, tile), lambda i, core: (0, core[0] * steps + i)),
            ],
            out_specs=[pl.BlockSpec((units, tile), lambda i, core: (0, i))] * 2,
        ),
        out_shape=[shape, shape],
        compiler_params=pltpu.CompilerParams(vmem_limit_bytes=16 * 1024 * 1024),
        cost_estimate=SMALL,
        name="exit_half",
    )(core.reshape(1), down, down)


def entry_kernel(rows_ref, weight_ref, out_ref):
    for which in range(2):
        out_ref[which] = jnp.dot(
            rows_ref[...], weight_ref[which], preferred_element_type=jnp.float32
        )


def entry(rows, weight):
    return pl.pallas_call(
        entry_kernel,
        in_specs=[pl.BlockSpec(memory_space=pltpu.VMEM)] * 2,
        out_specs=pl.BlockSpec(memory_space=pltpu.VMEM),
        out_shape=jax.ShapeDtypeStruct((2, rows.shape[0], weight.shape[2]), jnp.float32),
        compiler_params=pltpu.CompilerParams(vmem_limit_bytes=16 * 1024 * 1024),
        cost_estimate=SMALL,
        name="entry_products",
    )(rows, weight)


def inner_kernel(own_ref, other_ref, out_ref):
    gate_value = own_ref[0] + other_ref[0]
    up_value = own_ref[1] + other_ref[1]
    silu = gate_value / (1.0 + jnp.exp(-gate_value))
    out_ref[...] = (silu * up_value).astype(out_ref.dtype)


def inner_units(own, other, vmem=12):
    return pl.pallas_call(
        inner_kernel,
        in_specs=[pl.BlockSpec(memory_space=pltpu.VMEM)] * 2,
        out_specs=pl.BlockSpec(memory_space=pltpu.VMEM),
        out_shape=jax.ShapeDtypeStruct(own.shape[1:], jnp.bfloat16),
        compiler_params=pltpu.CompilerParams(vmem_limit_bytes=vmem * 1024 * 1024),
        cost_estimate=SMALL,
        name="inner_units",
    )(own, other)


def exit_kernel(own_ref, other_ref, down_own_ref, down_other_ref, *out_refs, sets, rows, sent):
    quarter = down_own_ref.shape[1] // 2
    tile = math.gcd(quarter, 256)

    def picked(ref, second):
        strips = []
        for begin, slots in sets:
            for slot in range(slots):
                for other in range(2):
                    y, x = (other, sent) if second else (sent, other)
                    at = ((begin + slot) * 4 + y * 2 + x) * rows
                    strips.append(ref[at : at + rows])
        return jnp.concatenate(strips, 0)

    for second in range(2):
        own, other = picked(own_ref, second), picked(other_ref, second)
        for at in range(quarter // tile):
            source = slice(second * quarter + at * tile, second * quarter + (at + 1) * tile)
            columns = slice(at * tile, (at + 1) * tile)
            part = jnp.dot(own, down_own_ref[:, source], preferred_element_type=jnp.float32)
            part += jnp.dot(other, down_other_ref[:, source], preferred_element_type=jnp.float32)
            row = 0
            for number, (_, slots) in enumerate(sets):
                target = out_refs[2 * number + second]
                for slot in range(slots):
                    for which in range(2):
                        value = part[row : row + rows]
                        target[which, slot, :, columns] = value.astype(target.dtype)
                        row += rows


def exit_sums(inner, down, rows, sets, sent):
    quarter = down[0].shape[1] // 2
    dtype = jnp.bfloat16 if sent else jnp.float32
    shapes = []
    for _, slots in sets:
        shapes += [jax.ShapeDtypeStruct((2, slots, rows, quarter), dtype)] * 2
    outs = pl.pallas_call(
        functools.partial(exit_kernel, sets=sets, rows=rows, sent=int(sent)),
        in_specs=[pl.BlockSpec(memory_space=pltpu.VMEM)] * 4,
        out_specs=[pl.BlockSpec(memory_space=pltpu.VMEM)] * len(shapes),
        out_shape=shapes,
        compiler_params=pltpu.CompilerParams(vmem_limit_bytes=16 * 1024 * 1024),
        cost_estimate=SMALL,
        name="exit_sums",
    )(*inner, *down)
    return [tuple(outs[at : at + 2]) for at in range(0, len(outs), 2)]


def after(value, *others):
    return lax.optimization_barrier((value,) + others)[0]


def on_device(
    hidden,
    expert_ids,
    route_weights,
    gate_weight,
    up_weight,
    down_weight,
    queries,
    latent_cache,
    lengths,
):
    devices = lax.axis_size(AXIS)
    planes = devices // SLICES
    me = lax.axis_index(AXIS)
    core, plane = lax.rem(me, 2), lax.div(me, SLICES)
    rows, width = hidden.shape
    half, quarter = width // 2, width // 4
    first_core = core == 0

    def swap(value, bit):
        return lax.ppermute(value, AXIS, [(i, i ^ bit) for i in range(devices)])

    def shift(value, by):
        return lax.ppermute(
            value, AXIS, [(i, (i + SLICES * by) % devices) for i in range(devices)]
        )

    in_core = functools.partial(swap, bit=1)
    in_x = functools.partial(swap, bit=2)
    in_y = functools.partial(swap, bit=4)

    low, high = hidden[:, :half], hidden[:, half:]
    kept = jnp.where(first_core, low, high)
    got = in_core(jnp.where(first_core, high, low))
    block = jnp.where(
        first_core, jnp.concatenate([kept, got], 0), jnp.concatenate([got, kept], 0)
    )
    choose = (
        expert_ids[:, :, None] == jnp.arange(planes, dtype=jnp.int32)[None, None, :]
    ).astype(jnp.float32)
    mixing = jnp.sum(route_weights[:, :, None] * choose, axis=1)
    mixing_other = in_core(mixing)
    mixing = jnp.where(
        first_core,
        jnp.concatenate([mixing, mixing_other], 0),
        jnp.concatenate([mixing_other, mixing], 0),
    )

    def mixing_of(expert):
        pick = jnp.arange(planes)[None, :] == expert
        return jnp.sum(jnp.where(pick, mixing, 0.0), axis=1, keepdims=True)

    queries_turned = jnp.swapaxes(queries, 1, 2)
    cache_turned = jnp.swapaxes(latent_cache, 1, 2)
    step = rows // ATTEND_CALLS

    def attend_more(number, held, *others):
        return attend(
            queries_turned, cache_turned, after(lengths, *others), number * step, step, held
        )

    def spread_first(slots):
        part_a = jnp.stack([slot[:, :quarter] for slot in slots])
        part_b = jnp.stack([slot[:, quarter:] for slot in slots])
        return (part_a, part_b), (in_x(part_a), in_y(part_b))

    def spread_second(held, got):
        pair_a = jnp.stack([held[0], got[0]])
        pair_b = jnp.stack([held[1], got[1]])
        return (pair_a, pair_b), (in_y(pair_a), in_x(pair_b))

    def spread_rows(held, got):
        four_a = jnp.stack([held[0], got[0]])
        four_b = jnp.stack([held[1], got[1]], 1)
        four = jnp.concatenate([four_a, four_b], -1)
        return jnp.moveaxis(four, 2, 0).reshape(-1, half)

    def narrow(value):
        return value.astype(jnp.bfloat16)

    def widen(value):
        return value.astype(jnp.float32)

    gate_part, up_part, down_part = gate_weight[0], up_weight[0], down_weight[0]

    def gather_second(kept, got):
        pair_a, pair_b = kept[0] + widen(got[0]), kept[1] + widen(got[1])
        return (pair_a[0], pair_b[0]), (narrow(pair_a[1]), narrow(pair_b[1]))

    def gather_rows(kept, got):
        return jnp.concatenate([kept[0] + widen(got[0]), kept[1] + widen(got[1])], -1)

    def returned(sums, slots):
        return [
            (k, sums[at] if k == 0 else shift(narrow(sums[at]), -k))
            for at, k in enumerate(slots)
        ]

    early = [planes - 1, 1]
    late = list(range(2, planes - 1))
    own_set, early_set, late_set = (0, 1), (1, len(early)), (0, len(late))
    join = lax.optimization_barrier

    def send_first(sent):
        return in_y(sent[0]), in_x(sent[1])

    def send_second(sent):
        return in_x(sent[0]), in_y(sent[1])

    slot_early = [shift(block, k) for k in early]
    held, got = spread_first([block])
    core, _ = join((core, block))
    core = hold(core)
    held, got, block, core = join((held, got, block, core))

    own, own_got = spread_second(held, got)
    entry_give, entry_own = entry_half(core, gate_part, up_part)
    own, own_got, slot_early, block, entry_give, entry_own = join(
        (own, own_got, slot_early, block, entry_give, entry_own)
    )
    entry_other = in_core(entry_give)

    slot_late = [shift(block, k) for k in late]
    held, got = spread_first(slot_early)
    shares = [mixing_of(lax.rem(plane + k, planes)) for k in range(planes)]
    held, got, shares = join((held, got, shares))

    early_held, early_got = spread_second(held, got)
    down_give, down_own = exit_half(after(core, *held), down_part)
    held, got = spread_first(slot_late)
    early_held, early_got, held, got, down_give, down_own = join(
        (early_held, early_got, held, got, down_give, down_own)
    )

    down = (down_own, in_core(down_give))
    arrived = jnp.concatenate(
        [spread_rows(own, own_got), spread_rows(early_held, early_got)], 0
    )
    pre_other = entry(arrived, entry_other)
    late_held, late_got = spread_second(held, got)
    pre_own = entry(arrived, entry_own)
    inner = inner_units(pre_own, in_core(pre_other))
    inner = (inner, in_core(inner))
    (sent,) = exit_sums(inner, down, 2 * rows, [early_set], True)
    late_held, late_got, sent, inner = join((late_held, late_got, sent, inner))

    got = send_first(sent)
    arrived = spread_rows(late_held, late_got)
    pre_other = entry(arrived, entry_other)
    pre_own = entry(arrived, entry_own)
    (kept,) = exit_sums(inner, down, 2 * rows, [early_set], False)
    (own_sent,) = exit_sums(inner, down, 2 * rows, [own_set], True)
    (own_kept,) = exit_sums(inner, down, 2 * rows, [own_set], False)
    attended = attend_more(0, None, *sent)
    kept, got, own_sent, own_kept, pre_own, pre_other, attended = join(
        (kept, got, own_sent, own_kept, pre_own, pre_other, attended)
    )

    kept, sent = gather_second(kept, got)
    got = send_second(sent)
    inner = inner_units(pre_own, in_core(pre_other))
    inner = (inner, in_core(inner))
    (late_sent,) = exit_sums(inner, down, 2 * rows, [late_set], True)
    (late_kept,) = exit_sums(inner, down, 2 * rows, [late_set], False)
    kept, got, late_sent, late_kept = join((kept, got, late_sent, late_kept))

    terms = returned(gather_rows(kept, got), early)
    got = send_first(late_sent)
    attended = attend_more(1, attended, *late_sent)
    late_kept, got, attended, own_sent = join((late_kept, got, attended, own_sent))

    kept, sent = gather_second(late_kept, got)
    got = send_second(sent)
    attended = attend_more(2, attended, *sent)
    kept, got, attended = join((kept, got, attended))

    terms += returned(gather_rows(kept, got), late)
    got = send_first(own_sent)
    attended = attend_more(3, attended, *kept)
    own_kept, got, attended = join((own_kept, got, attended))

    kept, sent = gather_second(own_kept, got)
    got = send_second(sent)
    terms += returned(gather_rows(kept, got), [0])
    slots = [k for k, _ in terms]
    terms, attended = join(([term for _, term in terms], attended))
    terms = list(zip(slots, terms))
    total = 0.0
    for k, term in terms:
        total = total + shares[k] * widen(term)

    result = narrow(total)
    top, bottom = result[:rows], result[rows:]
    kept = jnp.where(first_core, top, bottom)
    got = in_core(jnp.where(first_core, bottom, top))
    routed = jnp.where(
        first_core, jnp.concatenate([kept, got], 1), jnp.concatenate([got, kept], 1)
    )
    return routed, attended


def solution(mesh):
    in_specs = (
        P(("groups", "expert"), None),
        P(("groups", "expert"), None),
        P(("groups", "expert"), None),
        P("expert", None, None),
        P("expert", None, None),
        P("expert", None, None),
        P(("groups", "expert"), None, None),
        P(("groups", "expert"), None, None),
        P(("groups", "expert")),
    )
    out_specs = (P(("groups", "expert"), None), P(("groups", "expert"), None, None))
    return jax.shard_map(
        on_device, mesh=mesh, in_specs=in_specs, out_specs=out_specs, check_vma=False
    )
```
